32 devices in a mesh: dp: 4 (over y, core), fsdp: 8 (over z, x).
Axes of the slice: x: 2, y: 2, z: 4, core: 2. Of those that a mesh axis runs over, the one named last changes fastest.
Arguments:
- hidden_states: bfloat16 [16384, 1280], P(('dp', 'fsdp')), may hold values from -9 to 9
- clip_lengths: int32 [8], replicated, may hold values from 512 to 2048, as said below
- norm_gains: float32 [2, 1280], replicated, may hold values from 0.25 to 1.75
- norm_shifts: float32 [2, 1280], replicated, may hold values from -1.5 to 1.5
- proj_biases: float32 [4, 1280], replicated, may hold values from -1 to 1
- up_bias: float32 [5120], replicated, may hold values from -1.5 to 1.5
- in_proj: bfloat16 [3840, 1280], P('fsdp'), may hold values from -0.15625 to 0.15625
- out_proj: bfloat16 [1280, 1280], P('fsdp'), may hold values from -0.3125 to 0.3125
- up_proj: bfloat16 [5120, 1280], P('fsdp'), may hold values from -0.15625 to 0.15625
- down_proj: bfloat16 [1280, 5120], P('fsdp'), may hold values from -0.078125 to 0.078125
- cotangent: bfloat16 [16384, 1280], P(('dp', 'fsdp')), may hold values from -6 to 6
Outputs:
- layer_out: bfloat16 [16384, 1280], P(('dp', 'fsdp'))
- grad_hidden: bfloat16 [16384, 1280], P(('dp', 'fsdp'))
- grad_in_proj: float32 [3840, 1280], P('fsdp')
- grad_out_proj: float32 [1280, 1280], P('fsdp')
- grad_up_proj: float32 [5120, 1280], P('fsdp')
- grad_down_proj: float32 [1280, 5120], P('fsdp')
- grad_gains: float32 [2, 1280], replicated
- grad_shifts: float32 [2, 1280], replicated
- grad_biases: float32 [4, 1280], replicated
- grad_up_bias: float32 [5120], replicated
- root_means: float32 [3], replicated
The draws below stay inside these ranges and needn't reach their ends.
Inputs may be any that keep to these rules, and one draw needn't show every extreme that they name: Clip c owns the 2048 slots from c * 2048 on; its first clip_lengths[c] slots hold frames, the rest padding. Some clip fills all its slots in every draw.
All inputs are finite; a program needn't handle non-finite values.
Results may differ from the reference program's by a relative error of at most 0.015.
Values may be sent and summed in bfloat16 or wider, within the bound.
No kernel may reach another device: no remote copies, remote signals or barrier semaphores. Data moves between devices by JAX's collectives and lax.ppermute only.
A program may use at most 384 MiB of HBM per device.

```python
import jax
import jax.numpy as jnp
from jax import lax

D = 1280
H = 16
HD = 80
FF = 5120
TOK_DEV = 512
CLIP_DEV = 4
REGION = 2048
TOKENS = 16384
CLIPS = 8


def draw_hidden_states(key, part):
    key = jax.random.fold_in(key, 11)
    ramp = jnp.linspace(0.0, 1.0, TOKENS, dtype=jnp.float32)[:, None]
    base = jax.random.normal(key, (TOKENS, D), jnp.float32)
    return (jnp.clip(base, -5.0, 5.0) * (0.6 + 1.2 * ramp)).astype(jnp.bfloat16)


def draw_clip_lengths(key, part):
    key = jax.random.fold_in(key, 23)
    key_lengths, key_full = jax.random.split(key)
    region_span = CLIP_DEV * TOK_DEV
    lengths = jax.random.randint(key_lengths, (CLIPS,), region_span // 4, region_span + 1)
    full_index = jax.random.randint(key_full, (1,), 0, CLIPS)
    return jnp.where(jnp.arange(CLIPS) == full_index[0], region_span, lengths).astype(jnp.int32)


def with_spikes(result, rng, source, target, parts, factor):
    owner, partner = [(jnp.arange(result.shape[axis_at]) // (result.shape[axis_at] // parts)).reshape([-1 if axis == axis_at else 1 for axis in range(result.ndim)]) for axis_at in (source, target)]
    chosen = jax.random.permutation(rng, parts)[partner]
    strong = (owner == chosen) | (owner == (partner + parts // 2) % parts)
    return jnp.where(strong, factor * result, result)


def block_levels(rng, extent, shards, smallest, high):
    def one(axis_at, parts):
        draws = jax.random.uniform(jax.random.fold_in(jax.random.fold_in(rng, 6), axis_at), (parts,), jnp.float32, smallest / len(shards), high / len(shards))
        return jnp.repeat(jnp.exp(draws), extent[axis_at] // parts).reshape((-1,) + (1,) * (len(extent) - axis_at - 1))

    loudness = one(*shards[0])
    for cut in shards[1:]:
        loudness = loudness * one(*cut)
    return loudness


def bell_draw(rng, dims, scale, bound, shards=(), kind=jnp.bfloat16):
    gain = block_levels(rng, dims, shards, -0.22, 0.18) if shards else 1.0
    entries = jax.random.normal(rng, dims, jnp.float32) * scale * gain
    return jnp.minimum(jnp.maximum(entries, -bound), bound).astype(kind)


def bell_draw_with(key, dims, deviation, bound, pieces, heavy, kind=jnp.bfloat16):
    result = deviation * jax.random.normal(key, dims, jnp.float32)
    if pieces:
        result = result * block_levels(key, dims, pieces, -0.22, 0.18)
    return jnp.clip(with_spikes(result, jax.random.fold_in(key, 3), *heavy), -bound, bound).astype(kind)


def setup_inputs(seed: int = 0) -> dict:
    streams_of = jax.random.split(jax.random.key(seed), 12)
    return {
        "hidden_states": draw_hidden_states(jax.random.fold_in(streams_of[11], 71), 0),
        "clip_lengths": draw_clip_lengths(jax.random.fold_in(streams_of[11], 71), 0),
        "norm_gains": jnp.clip(1.0 + 0.15 * jax.random.normal(streams_of[2], (2, D), jnp.float32), 0.25, 1.75),
        "norm_shifts": bell_draw(streams_of[3], (2, D), 0.3, 1.5, (), jnp.float32),
        "proj_biases": bell_draw(streams_of[4], (4, D), 0.2, 1.0, (), jnp.float32),
        "up_bias": bell_draw(streams_of[5], (FF,), 0.3, 1.5, (), jnp.float32),
        "in_proj": bell_draw(streams_of[6], (3 * D, D), D ** -0.5, 0.15625, ((0, 8),)),
        "out_proj": bell_draw(streams_of[7], (D, D), (D // 4) ** -0.5, 0.3125, ((0, 8),)),
        "up_proj": bell_draw(streams_of[8], (FF, D), D ** -0.5, 0.15625, ((0, 8),)),
        "down_proj": bell_draw(streams_of[9], (D, FF), FF ** -0.5, 0.078125, ((0, 8),)),
        "cotangent": bell_draw_with(streams_of[10], (TOKENS, D), 1.0, 6.0, ((0, 32),), (0, 1, 32, 2.75)),
    }


@jax.custom_vjp
def low(v):
    return lax.optimization_barrier(v.astype(jnp.bfloat16)).astype(jnp.float32)

@jax.custom_vjp
def low_back(v):
    return v

def low_keep(v):
    return (low(v), None)

def low_pass(kept, grad):
    return (grad,)

def back_keep(v):
    return (v, None)

def back_low(kept, grad):
    return (low(grad),)
low.defvjp(low_keep, low_pass)
low_back.defvjp(back_keep, back_low)
epsilon = 1e-05
highest = lax.Precision.HIGHEST

def norm_rows(values, gain_row, shift_row):
    center = values - lax.optimization_barrier(jnp.mean(values, axis=-1, keepdims=True))
    spread = lax.optimization_barrier(jnp.mean(center * center, axis=-1, keepdims=True))
    return center * lax.rsqrt(spread + epsilon) * gain_row + shift_row

def times_rows(operand, weight):
    return jnp.einsum('ni,oi->no', operand, weight, precision=highest)

def region_layer(region_rows, length, norm_gains, norm_shifts, proj_biases, up_bias, in_proj, out_proj, up_proj, down_proj):
    normed_one = low(norm_rows(region_rows, norm_gains[0], norm_shifts[0]))
    projected = times_rows(normed_one, in_proj)
    queries = low(low_back(projected[:, :D] + proj_biases[0]))
    keys_all = low(low_back(projected[:, D:2 * D]))
    values_all = low(low_back(projected[:, 2 * D:] + proj_biases[1]))
    scores = jnp.einsum('qhd,khd->hqk', queries.reshape(REGION, H, HD), keys_all.reshape(REGION, H, HD), precision=highest) * HD ** (-0.5)
    scores = low_back(scores)
    key_valid = jnp.arange(REGION, dtype=jnp.int32) < length
    scores = jnp.where(key_valid[None, None, :], scores, -1e+30)
    weights_soft = low(jax.nn.softmax(scores, axis=-1))
    context = jnp.einsum('hqk,khd->qhd', weights_soft, values_all.reshape(REGION, H, HD), precision=highest).reshape(REGION, D)
    context = low(low_back(context))
    attention = low_back(times_rows(context, out_proj) + proj_biases[2])
    middle = region_rows + attention
    normed_two = low(norm_rows(middle, norm_gains[1], norm_shifts[1]))
    widened = low_back(times_rows(normed_two, up_proj) + up_bias)
    activated = low(jax.nn.gelu(widened, approximate=False))
    feedforward = times_rows(activated, down_proj) + proj_biases[3]
    row_valid = key_valid.astype(jnp.float32)
    stat_terms = jnp.stack([jnp.sum(row_valid * lax.optimization_barrier(jnp.sum(middle * middle, axis=1))), jnp.sum(row_valid * lax.optimization_barrier(jnp.sum(attention * attention, axis=1))), jnp.sum(row_valid * lax.optimization_barrier(jnp.sum(feedforward * feedforward, axis=1)))])
    return (middle + feedforward, stat_terms)

def whole_layer(hidden_float, norm_gains, norm_shifts, proj_biases, up_bias, in_proj, out_proj, up_proj, down_proj, clip_lengths):
    layer_step = jax.checkpoint(region_layer)

    def scan_step(stat_total, item_pair):
        region_out, stat_terms = layer_step(item_pair[0], item_pair[1], norm_gains, norm_shifts, proj_biases, up_bias, in_proj, out_proj, up_proj, down_proj)
        return (stat_total + stat_terms, region_out)
    stat_total, region_outs = lax.scan(scan_step, jnp.zeros((3,), jnp.float32), (hidden_float.reshape(CLIPS, REGION, D), clip_lengths))
    return (region_outs.reshape(TOKENS, D), stat_total)

def reference(hidden_states, clip_lengths, norm_gains, norm_shifts, proj_biases, up_bias, in_proj, out_proj, up_proj, down_proj, cotangent):

    def layer_only(hidden_float, gains_all, shifts_all, biases_all, bias_wide, in_float, out_float, up_float, down_float):
        return whole_layer(hidden_float, gains_all, shifts_all, biases_all, bias_wide, in_float, out_float, up_float, down_float, clip_lengths)
    outputs, pullback, stat_total = jax.vjp(layer_only, hidden_states.astype(jnp.float32), norm_gains, norm_shifts, proj_biases, up_bias, in_proj.astype(jnp.float32), out_proj.astype(jnp.float32), up_proj.astype(jnp.float32), down_proj.astype(jnp.float32), has_aux=True)
    grads = pullback(cotangent.astype(jnp.float32))
    valid_count = jnp.sum(clip_lengths).astype(jnp.float32) * D
    root_means = jnp.sqrt(stat_total / valid_count)
    return (outputs.astype(jnp.bfloat16), grads[0].astype(jnp.bfloat16), grads[5], grads[6], grads[7], grads[8], grads[1], grads[2], grads[3], grads[4], root_means)
```

```python
import functools
import math

import jax
import jax.numpy as jnp
from jax import lax
from jax.experimental import pallas as pl
from jax.experimental.pallas import tpu as pltpu
from jax.sharding import PartitionSpec as P

H = 16
HD = 80
CLIP_DEV = 4
LANES = 128
GROUP_HEADS = H // CLIP_DEV
EPSILON = 1e-05
SCORE_SCALE = HD ** (-0.5) * math.log2(math.e)
LN2 = math.log(2.0)
LOW = jnp.bfloat16
QUERY_BLOCK = 256
GRAD_BLOCK = 256
VMEM_BYTES = 56 * 1024 * 1024


def swap(value, axis, mask):
    pairs = [(source, source ^ mask) for source in range(lax.axis_size(axis))]
    return lax.ppermute(value, axis, pairs)


def dot_nt(lhs, rhs):
    return lax.dot_general(
        lhs, rhs, (((1,), (1,)), ((), ())), preferred_element_type=jnp.float32
    )


def dot_nn(lhs, rhs):
    return jnp.dot(lhs, rhs, preferred_element_type=jnp.float32)


def dot_tn(lhs, rhs):
    return lax.dot_general(
        lhs, rhs, (((0,), (0,)), ((), ())), preferred_element_type=jnp.float32
    )


def split_three(value):
    high = value.astype(LOW).astype(jnp.float32)
    rest = value - high
    middle = rest.astype(LOW).astype(jnp.float32)
    return high, middle, rest - middle


def with_lanes(block, first, columns):
    lane = lax.broadcasted_iota(jnp.int32, block.shape, 1)
    for place, column in enumerate(columns):
        block = jnp.where(lane == first + place, column, block)
    return block


def attend_kernel(query_ref, key_ref, value_ref, context_ref, query_out_ref):
    queries = query_ref[...]
    scores = dot_nt(queries, key_ref[...])
    largest = jnp.max(scores, axis=1, keepdims=True)
    exponent = jnp.exp2(scores - largest)
    mixed = dot_nn(exponent.astype(LOW), value_ref[...])
    summed = mixed[:, HD : HD + 1]
    context_ref[...] = (mixed / summed).astype(LOW)
    log_parts = split_three(-(largest + jnp.log2(summed)))
    query_out_ref[...] = with_lanes(
        queries.astype(jnp.float32), HD + 1, log_parts
    ).astype(LOW)


def attend(projected):
    rows = projected.shape[0]
    block = min(QUERY_BLOCK, rows)
    out = jax.ShapeDtypeStruct((rows, GROUP_HEADS * LANES), LOW)
    whole = pl.BlockSpec((rows, LANES), lambda head, step: (0, GROUP_HEADS + head))
    return pl.pallas_call(
        attend_kernel,
        grid=(GROUP_HEADS, rows // block),
        in_specs=[
            pl.BlockSpec((block, LANES), lambda head, step: (step, head)),
            whole,
            pl.BlockSpec((rows, LANES), lambda head, step: (0, 2 * GROUP_HEADS + head)),
        ],
        out_specs=[pl.BlockSpec((block, LANES), lambda head, step: (step, head))] * 2,
        out_shape=[out, out],
        compiler_params=pltpu.CompilerParams(vmem_limit_bytes=VMEM_BYTES),
        cost_estimate=pl.CostEstimate(
            flops=8 * GROUP_HEADS * rows * rows * LANES,
            bytes_accessed=5 * rows * GROUP_HEADS * LANES * 2,
            transcendentals=GROUP_HEADS * rows * rows,
        ),
    )(projected, projected, projected)


def attend_back_kernel(
    query_ref,
    key_ref,
    value_ref,
    context_ref,
    grad_ref,
    grad_query_ref,
    grad_key_ref,
    grad_value_ref,
    key_turned,
    key_total,
    value_total,
):
    step = pl.program_id(1)

    @pl.when(step == 0)
    def _():
        key_turned[...] = key_ref[...].T
        key_total[...] = jnp.zeros_like(key_total)
        value_total[...] = jnp.zeros_like(value_total)

    queries = query_ref[...]
    grad = grad_ref[...]
    grad_float = grad.astype(jnp.float32)
    row_term = jnp.sum(grad_float * context_ref[...].astype(jnp.float32), axis=1, keepdims=True)
    grad = with_lanes(grad_float, HD, split_three(-row_term)).astype(LOW)
    soft = jnp.exp2(dot_nt(key_ref[...], queries))
    grad_soft = dot_nt(value_ref[...], grad)
    value_total[...] += dot_nn(soft.astype(LOW), grad)
    grad_scores = (soft * grad_soft).astype(LOW)
    key_total[...] += dot_nn(grad_scores, queries)
    grad_query = dot_nn(key_turned[...], grad_scores)
    grad_query_ref[...] = (grad_query * HD ** (-0.5)).T.astype(LOW)

    @pl.when(step == pl.num_programs(1) - 1)
    def _():
        grad_key_ref[...] = (key_total[...] * LN2).astype(LOW)
        grad_value_ref[...] = value_total[...].astype(LOW)


def attend_back(queries, projected, context, grad_context):
    rows = projected.shape[0]
    block = min(GRAD_BLOCK, rows)
    out = jax.ShapeDtypeStruct((rows, GROUP_HEADS * LANES), LOW)
    part = pl.BlockSpec((block, LANES), lambda head, step: (step, head))
    whole = pl.BlockSpec((rows, LANES), lambda head, step: (0, head))
    return pl.pallas_call(
        attend_back_kernel,
        grid=(GROUP_HEADS, rows // block),
        in_specs=[
            part,
            pl.BlockSpec((rows, LANES), lambda head, step: (0, GROUP_HEADS + head)),
            pl.BlockSpec((rows, LANES), lambda head, step: (0, 2 * GROUP_HEADS + head)),
            part,
            part,
        ],
        out_specs=[part, whole, whole],
        out_shape=[out] * 3,
        scratch_shapes=[
            pltpu.VMEM((LANES, rows), LOW),
            pltpu.VMEM((rows, LANES), jnp.float32),
            pltpu.VMEM((rows, LANES), jnp.float32),
        ],
        compiler_params=pltpu.CompilerParams(vmem_limit_bytes=VMEM_BYTES),
        cost_estimate=pl.CostEstimate(
            flops=20 * GROUP_HEADS * rows * rows * LANES,
            bytes_accessed=8 * rows * GROUP_HEADS * LANES * 2,
            transcendentals=GROUP_HEADS * rows * rows,
        ),
    )(queries, projected, projected, context, grad_context)


def normalise(values):
    center = values - jnp.mean(values, axis=-1, keepdims=True)
    spread = jnp.mean(center * center, axis=-1, keepdims=True)
    scale = lax.rsqrt(spread + EPSILON)
    return center * scale, scale


def norm_back(grad, gain, unit, scale):
    scaled = grad * gain
    return scale * (
        scaled
        - jnp.mean(scaled, axis=-1, keepdims=True)
        - unit * jnp.mean(scaled * unit, axis=-1, keepdims=True)
    )


def gelu_exact(values):
    return jax.nn.gelu(values, approximate=False)


def pick(blocks, index, axis=0):
    return lax.dynamic_index_in_dim(blocks, index, axis, keepdims=False)


def gather_bits(piece, bits):
    held = piece.reshape((1,) * len(bits) + piece.shape)
    for place in sorted(range(len(bits)), key=lambda i: bits[i][3]):
        axis, mask, mine, _ = bits[place]
        came = swap(held, axis, mask)
        held = jnp.where(
            mine == 1,
            jnp.concatenate([came, held], axis=place),
            jnp.concatenate([held, came], axis=place),
        )
    return held


def reduce_bits(held, bits):
    for place in sorted(range(len(bits)), key=lambda i: -bits[i][3]):
        axis, mask, mine, _ = bits[place]
        kept = lax.dynamic_slice_in_dim(held, mine, 1, place)
        sent = lax.dynamic_slice_in_dim(held, 1 - mine, 1, place)
        came = swap(sent, axis, mask)
        held = (kept.astype(jnp.float32) + came.astype(jnp.float32)).astype(LOW)
    return held.reshape(held.shape[len(bits) :])


def on_device(
    hidden_states,
    clip_lengths,
    norm_gains,
    norm_shifts,
    proj_biases,
    up_bias,
    in_proj,
    out_proj,
    up_proj,
    down_proj,
    cotangent,
):
    tokens_here, width = hidden_states.shape
    fsdp_count = lax.axis_size("fsdp")
    dp_count = lax.axis_size("dp")
    fsdp_index = lax.axis_index("fsdp")
    dp_index = lax.axis_index("dp")
    core = dp_index % 2
    copies = dp_count // 2
    copy_index = dp_index // 2
    region = (dp_index * fsdp_count + fsdp_index) // CLIP_DEV
    place = fsdp_index % CLIP_DEV
    length = lax.dynamic_index_in_dim(clip_lengths, region, keepdims=False)
    span = tokens_here * CLIP_DEV
    hidden_units = up_bias.shape[0]
    positions = jnp.arange(tokens_here, dtype=jnp.int32)
    row_valid = (place * tokens_here + positions < length).astype(jnp.float32)
    fsdp_levels = fsdp_count.bit_length() - 1
    copy_levels = copies.bit_length() - 1

    def bits_of(turn):
        bits = []
        for level in reversed(range(fsdp_levels)):
            when = fsdp_levels - level if level else (100 if turn else 300)
            bits.append(("fsdp", 1 << level, fsdp_index >> level & 1, when))
        for level in reversed(range(copy_levels)):
            bits.append(("dp", 2 << level, copy_index >> level & 1, 200 - level))
        return bits

    core_bit = ("dp", 1, core, 1000)

    with jax.named_scope("gather_tokens"):
        half = width // 2
        own_x = hidden_states
        near_a = swap(own_x[:, :half], "fsdp", 1)
        far_b = swap(own_x[:, half:], "fsdp", 2)
        far_a, both_a = swap((own_x[:, :half], near_a), "fsdp", 2)
        near_b, both_b = swap((own_x[:, half:], far_b), "fsdp", 1)
        clip_x = jnp.concatenate(
            [
                own_x,
                jnp.concatenate([near_a, near_b], axis=1),
                jnp.concatenate([far_a, far_b], axis=1),
                jnp.concatenate([both_a, both_b], axis=1),
            ]
        ).astype(jnp.float32)
    block_place = place ^ jnp.arange(CLIP_DEV, dtype=jnp.int32)
    clip_position = (block_place[:, None] * tokens_here + positions).reshape(span)
    key_mask = jnp.where(clip_position < length, 0.0, -1e30).astype(jnp.float32)

    with jax.named_scope("gather_in_proj"):
        rounds = fsdp_count // CLIP_DEV
        unit_rows = in_proj.shape[0] // 3
        half_rows = unit_rows // 2
        units = in_proj.reshape(3, 2, half_rows, width)
        own_units = pick(units, core, 1)

        def route(slot, turn):
            pairs = []
            for source in range(fsdp_count):
                unit = (3 * source + slot) % fsdp_count
                owner, spot = unit // rounds, unit % rounds
                pairs.append((source, owner + CLIP_DEV * ((spot + turn) % rounds)))
            return pairs

        came = jnp.stack(
            [
                jnp.stack([lax.ppermute(own_units[slot], "fsdp", route(slot, turn)) for turn in range(rounds)])
                for slot in range(3)
            ]
        )
        came = gather_bits(came, [core_bit])
        came = jnp.moveaxis(came, 0, 2).reshape(3, rounds, unit_rows, width)
        lap = fsdp_index // CLIP_DEV

        def slot_of(kind, spot):
            return (place * rounds + spot + kind * fsdp_count) % 3

        weight_rows = jnp.stack(
            [
                jnp.concatenate(
                    [
                        pick(pick(came, slot_of(kind, spot)), (lap - spot) % rounds)
                        for spot in range(rounds)
                    ]
                )
                for kind in range(3)
            ]
        )
        group_width = GROUP_HEADS * HD
        padded_width = 3 * GROUP_HEADS * LANES
        weight_in = jnp.pad(
            weight_rows.reshape(3 * GROUP_HEADS, HD, width), ((0, 0), (0, LANES - HD), (0, 0))
        ).reshape(padded_width, width)

    unit_one, scale_one = normalise(clip_x)
    normed_one = (unit_one * norm_gains[0] + norm_shifts[0]).astype(LOW)
    zeros = jnp.zeros((width,), jnp.float32)
    group_bias = jnp.stack([proj_biases[0], zeros, proj_biases[1]]).reshape(3, CLIP_DEV, GROUP_HEADS, HD)
    group_bias = jnp.pad(pick(group_bias, place, 1), ((0, 0), (0, 0), (0, LANES - HD)))
    lane = jnp.arange(LANES)
    kind_scale = jnp.array([SCORE_SCALE, 1.0, 1.0], jnp.float32)[:, None, None]
    spare = jnp.stack(
        [
            lane == HD,
            (lane > HD) & (lane <= HD + 3),
            (lane >= HD) & (lane < HD + 3),
        ]
    ).astype(jnp.float32)
    column_shift = (group_bias * kind_scale + spare[:, None]).reshape(padded_width)
    column_scale = jnp.broadcast_to(kind_scale, group_bias.shape).reshape(padded_width)
    mask_lane = jnp.broadcast_to(
        (jnp.arange(3)[:, None, None] == 1) & (lane == HD), group_bias.shape
    ).reshape(padded_width)
    projected = dot_nt(normed_one, weight_in) * column_scale + column_shift
    projected = jnp.where(mask_lane, key_mask[:, None], projected).astype(LOW)
    context_heads, queries_ready = attend(projected)

    def to_heads(blocks):
        return blocks

    with jax.named_scope("context_back"):
        compact = context_heads.reshape(CLIP_DEV, tokens_here, GROUP_HEADS, LANES)[..., :HD]
        compact = compact.reshape(CLIP_DEV, tokens_here, group_width)
        parts = [compact[0]] + [swap(compact[j], "fsdp", j) for j in range(1, CLIP_DEV)]
        parts = jnp.stack(parts)
        context_low = jnp.concatenate(
            [pick(parts, place ^ group) for group in range(CLIP_DEV)], axis=1
        )

    with jax.named_scope("gather_weights"):
        out_rows = out_proj.shape[0] // dp_count
        out_piece = pick(out_proj.reshape(copies, 2, out_rows, width), copy_index)
        out_piece = pick(out_piece, core)
        out_full = gather_bits(out_piece, bits_of(True) + [core_bit]).reshape(width, width)
        shard_units = up_proj.shape[0]
        half_units = shard_units // 2
        up_rows = half_units // copies
        up_piece = pick(up_proj.reshape(2, copies, up_rows, width), core)
        up_piece = pick(up_piece, copy_index)
        up_half = gather_bits(up_piece, bits_of(True)).reshape(hidden_units // 2, width)
        down_rows = down_proj.shape[0] // copies
        down_piece = pick(down_proj.reshape(copies, down_rows, fsdp_count, 2, half_units), copy_index)
        down_piece = pick(down_piece, core, 2).reshape(down_rows, hidden_units // 2)
        down_half = gather_bits(down_piece, bits_of(False)).reshape(width, hidden_units // 2)

    inputs = hidden_states.astype(jnp.float32)
    attention = dot_nt(context_low, out_full) + proj_biases[2]
    middle = inputs + attention
    unit_two, scale_two = normalise(middle)
    normed_two = (unit_two * norm_gains[1] + norm_shifts[1]).astype(LOW)
    normed_pair = jnp.concatenate([normed_two, swap(normed_two, "dp", 1)])
    grad_pair = jnp.concatenate([cotangent, swap(cotangent, "dp", 1)])
    half_bias = pick(up_bias.reshape(fsdp_count, 2, half_units), core, 1).reshape(hidden_units // 2)
    widened = dot_nt(normed_pair, up_half) + half_bias
    activated, gelu_back = jax.vjp(gelu_exact, widened)
    activated_low = activated.astype(LOW)
    grad_activated = dot_nn(grad_pair, down_half)
    grad_widened = gelu_back(grad_activated)[0].astype(LOW)

    def over_cores(partial):
        return partial[:tokens_here] + swap(partial[tokens_here:].astype(LOW), "dp", 1).astype(jnp.float32)

    feedforward = over_cores(dot_nt(activated_low, down_half)) + proj_biases[3]
    outputs = (middle + feedforward).astype(LOW)
    stat_terms = jnp.stack(
        [
            jnp.sum(row_valid * jnp.sum(middle * middle, axis=1)),
            jnp.sum(row_valid * jnp.sum(attention * attention, axis=1)),
            jnp.sum(row_valid * jnp.sum(feedforward * feedforward, axis=1)),
        ]
    )
    grad_normed_two = over_cores(dot_nn(grad_widened, up_half))
    grad_out = cotangent.astype(jnp.float32)
    grad_middle = grad_out + norm_back(grad_normed_two, norm_gains[1], unit_two, scale_two)
    grad_attention = grad_middle.astype(LOW)
    grad_context = dot_nn(grad_attention, out_full).astype(LOW)

    with jax.named_scope("grad_context_to_heads"):
        groups = jnp.moveaxis(grad_context.reshape(tokens_here, CLIP_DEV, group_width), 1, 0)
        sends = [pick(groups, place ^ j) for j in range(CLIP_DEV)]
        grad_heads = jnp.stack([sends[0]] + [swap(sends[j], "fsdp", j) for j in range(1, CLIP_DEV)])
        grad_heads = jnp.pad(
            grad_heads.reshape(span, GROUP_HEADS, HD), ((0, 0), (0, 0), (0, LANES - HD))
        ).reshape(span, GROUP_HEADS * LANES)

    grad_down = dot_tn(grad_pair, activated_low).astype(LOW)
    grad_up = dot_tn(grad_widened, normed_pair).astype(LOW)
    grad_exit = dot_tn(grad_attention, context_low).astype(LOW)

    def shape_of(bits):
        return (2,) * len(bits)

    with jax.named_scope("reduce_weights"):
        bits = bits_of(False)
        down_sum = reduce_bits(grad_down.reshape(shape_of(bits) + (down_rows, hidden_units // 2)), bits)
        bits = bits_of(True)
        up_sum = reduce_bits(grad_up.reshape(shape_of(bits) + (up_rows, width)), bits)
        bits = bits_of(True) + [core_bit]
        exit_sum = reduce_bits(grad_exit.reshape(shape_of(bits) + (out_rows, width)), bits)
        copy_bits = [bit for bit in bits_of(False) if bit[0] == "dp"]
        down_sum = gather_bits(down_sum, copy_bits + [core_bit])
        down_sum = down_sum.reshape(copies, 2, down_rows, fsdp_count, half_units)
        down_sum = jnp.moveaxis(down_sum, 1, 3).reshape(down_proj.shape).astype(jnp.float32)
        up_sum = gather_bits(up_sum, [core_bit] + copy_bits).reshape(up_proj.shape).astype(jnp.float32)
        exit_sum = gather_bits(exit_sum, copy_bits + [core_bit]).reshape(out_proj.shape).astype(jnp.float32)

    grad_query, grad_key, grad_value = attend_back(queries_ready, projected, context_heads, grad_heads)
    grad_projected = jnp.concatenate([grad_query, grad_key, grad_value], axis=1)
    partial_one = dot_nn(grad_projected, weight_in)
    gain_one = jnp.sum(partial_one * unit_one, axis=0)
    shift_one = jnp.sum(partial_one, axis=0)
    grad_entry = dot_tn(grad_projected, normed_one)
    grad_entry = grad_entry.reshape(3, GROUP_HEADS, LANES, width)[:, :, :HD].astype(LOW)

    with jax.named_scope("reduce_tokens"):
        blocks = partial_one.reshape(CLIP_DEV, tokens_here, width)
        first, second = blocks[:, :, :half], blocks[:, :, half:]
        came = swap(first[1::2].astype(LOW), "fsdp", 1)
        first = first[0::2] + came.astype(jnp.float32)
        first = first[0] + swap(first[1].astype(LOW), "fsdp", 2).astype(jnp.float32)
        came = swap(second[2:].astype(LOW), "fsdp", 2)
        second = second[:2] + came.astype(jnp.float32)
        second = second[0] + swap(second[1].astype(LOW), "fsdp", 1).astype(jnp.float32)
        grad_normed_one = jnp.concatenate([first, second], axis=1)

    with jax.named_scope("reduce_in_proj"):
        entry_bits = [core_bit] + copy_bits
        entry = grad_entry.reshape(3, rounds, 2, copies, half_rows // copies, width)
        entry = jnp.moveaxis(entry, (2, 3), (0, 1))
        entry = entry.reshape((2,) * len(entry_bits) + (3, rounds, half_rows // copies, width))
        entry = reduce_bits(entry, entry_bits)
        totals = []
        for slot in range(3):
            total = 0.0
            for turn in range(rounds):
                spot = (lap - turn) % rounds
                kind = ((slot - place * rounds - spot) * pow(fsdp_count, -1, 3)) % 3
                sent = pick(pick(entry, kind), spot)
                back = [(target, source) for source, target in route(slot, turn)]
                total = total + lax.ppermute(sent, "fsdp", back).astype(jnp.float32)
            totals.append(total.astype(LOW))
        entry_sum = gather_bits(jnp.stack(totals), entry_bits)
        entry_sum = entry_sum.reshape(2, copies, 3, half_rows // copies, width)
        entry_sum = jnp.moveaxis(entry_sum, 2, 0).reshape(in_proj.shape).astype(jnp.float32)

    grad_hidden = grad_middle + norm_back(grad_normed_one, norm_gains[0], unit_one[:tokens_here], scale_one[:tokens_here])

    def place_heads(grads):
        columns = jnp.sum(grads.astype(jnp.float32), axis=0).reshape(GROUP_HEADS, LANES)[:, :HD]
        rows = jnp.zeros((CLIP_DEV, group_width), jnp.float32)
        return lax.dynamic_update_index_in_dim(rows, columns.reshape(group_width), place, 0).reshape(width)

    bias_terms = jnp.stack(
        [
            place_heads(grad_query),
            place_heads(grad_value),
            jnp.sum(grad_attention.astype(jnp.float32), axis=0),
            jnp.sum(grad_out, axis=0),
        ]
    )
    half_up = jnp.sum(grad_widened.astype(jnp.float32), axis=0).reshape(fsdp_count, half_units)
    up_terms = jnp.zeros((fsdp_count, 2, half_units), jnp.float32)
    up_terms = lax.dynamic_update_index_in_dim(up_terms, half_up, core, 1).reshape(hidden_units)
    small_totals = lax.psum(
        (
            jnp.stack([gain_one, jnp.sum(grad_normed_two * unit_two, axis=0)]),
            jnp.stack([shift_one, jnp.sum(grad_normed_two, axis=0)]),
            bias_terms,
            up_terms,
            stat_terms,
        ),
        ("dp", "fsdp"),
    )
    valid_count = jnp.sum(clip_lengths).astype(jnp.float32) * width
    root_means = jnp.sqrt(small_totals[4] / valid_count)
    return (
        outputs,
        grad_hidden.astype(LOW),
        entry_sum,
        exit_sum,
        up_sum,
        down_sum,
        small_totals[0],
        small_totals[1],
        small_totals[2],
        small_totals[3],
        root_means,
    )


def solution(mesh):
    in_specs = (
        P(("dp", "fsdp"), None),
        P(),
        P(),
        P(),
        P(),
        P(),
        P("fsdp", None),
        P("fsdp", None),
        P("fsdp", None),
        P("fsdp", None),
        P(("dp", "fsdp"), None),
    )
    out_specs = (
        P(("dp", "fsdp"), None),
        P(("dp", "fsdp"), None),
        P("fsdp", None),
        P("fsdp", None),
        P("fsdp", None),
        P("fsdp", None),
        P(),
        P(),
        P(),
        P(),
        P(),
    )
    return jax.shard_map(
        on_device, mesh=mesh, in_specs=in_specs, out_specs=out_specs, check_vma=False
    )
```

```python
import functools
import math

import jax
import jax.numpy as jnp
from jax import lax
from jax.experimental import pallas as pl
from jax.experimental.pallas import tpu as pltpu
from jax.sharding import PartitionSpec as P

H = 16
HD = 80
CLIP_DEV = 4
LANES = 128
GROUP_HEADS = H // CLIP_DEV
EPSILON = 1e-05
SCORE_SCALE = HD ** (-0.5) * math.log2(math.e)
LN2 = math.log(2.0)
LOW = jnp.bfloat16
TOKEN_BLOCK = 256
QUERY_BLOCK = 256
GRAD_BLOCK = 256
UNIT_BLOCK = 512
GROUP_LANES = GROUP_HEADS * LANES
GROUP_WIDTH = GROUP_HEADS * HD
VMEM_BYTES = 56 * 1024 * 1024


def swap(value, axis, mask):
    pairs = [(source, source ^ mask) for source in range(lax.axis_size(axis))]
    return lax.ppermute(value, axis, pairs)


def dot_nt(lhs, rhs):
    return lax.dot_general(
        lhs, rhs, (((1,), (1,)), ((), ())), preferred_element_type=jnp.float32
    )


def dot_nn(lhs, rhs):
    return jnp.dot(lhs, rhs, preferred_element_type=jnp.float32)


def dot_tn(lhs, rhs):
    return lax.dot_general(
        lhs, rhs, (((0,), (0,)), ((), ())), preferred_element_type=jnp.float32
    )


def split_three(value):
    high = value.astype(LOW).astype(jnp.float32)
    rest = value - high
    middle = rest.astype(LOW).astype(jnp.float32)
    return high, middle, rest - middle


def with_lanes(block, first, columns):
    lane = lax.broadcasted_iota(jnp.int32, block.shape, 1)
    for place, column in enumerate(columns):
        block = jnp.where(lane == first + place, column, block)
    return block


def divisor(size, most):
    block = min(size, most)
    while size % block:
        block //= 2
    return block


ANYWHERE = pl.BlockSpec(memory_space=pl.ANY)


def call(body, grid, scalars, inputs, outputs, held=None, scratch=(), cost=(0, 0, 0), after=()):
    held = () if held is None else tuple(held)
    passive = held + tuple(after)
    n_scalar, n_in, n_passive, n_out = len(scalars), len(inputs), len(passive), len(outputs)

    def kernel(*refs):
        first = n_scalar + n_in
        body(*refs[:first], *refs[first + n_passive :])

    flops, moved, special = cost
    return pl.pallas_call(
        kernel,
        grid_spec=pltpu.PrefetchScalarGridSpec(
            num_scalar_prefetch=n_scalar,
            grid=grid,
            in_specs=[spec for _, spec in inputs] + [ANYWHERE] * n_passive,
            out_specs=[spec for _, spec in outputs],
            scratch_shapes=list(scratch),
        ),
        out_shape=[shape for shape, _ in outputs],
        input_output_aliases={n_scalar + n_in + i: i for i in range(len(held))},
        compiler_params=pltpu.CompilerParams(vmem_limit_bytes=VMEM_BYTES),
        cost_estimate=pl.CostEstimate(flops=int(flops), bytes_accessed=int(moved), transcendentals=int(special)),
    )(*scalars, *(array for array, _ in inputs), *passive)


def like(rows, columns, kind=LOW):
    return jax.ShapeDtypeStruct((rows, columns), kind)


def whole_block(array):
    return pl.BlockSpec(array.shape, lambda *_: (0,) * len(array.shape))


def unit_rows_of(values):
    center = values - jnp.mean(values, axis=-1, keepdims=True)
    spread = jnp.mean(center * center, axis=-1, keepdims=True)
    return center * lax.rsqrt(spread + EPSILON)


def project_kernel(limit_ref, x_ref, weight_ref, gain_ref, shift_ref, column_ref, query_ref, pair_ref, normed_ref):
    rows = x_ref.shape[0]
    unit = unit_rows_of(x_ref[...].astype(jnp.float32))
    normed = (unit * gain_ref[...] + shift_ref[...]).astype(LOW)
    normed_ref[...] = normed
    columns = column_ref[...]
    queries = dot_nt(normed, weight_ref[:GROUP_LANES, :])
    query_ref[...] = (queries * SCORE_SCALE + columns[:, :GROUP_LANES]).astype(LOW)
    pair = dot_nt(normed, weight_ref[GROUP_LANES:, :]) + columns[:, GROUP_LANES:]
    row = pl.program_id(0) * rows + lax.broadcasted_iota(jnp.int32, pair.shape, 0)
    lane = lax.broadcasted_iota(jnp.int32, pair.shape, 1)
    masked = (row >= limit_ref[0]) & (lane % LANES == HD) & (lane < GROUP_LANES)
    pair_ref[...] = jnp.where(masked, -1e30, pair).astype(LOW)


def project(number, x_block, weight, gain, shift, columns, limit, held, after=()):
    tokens, width = x_block.shape
    block = divisor(tokens, TOKEN_BLOCK)
    steps = tokens // block
    rows = CLIP_DEV * tokens

    def out(columns_out):
        return like(rows, columns_out), pl.BlockSpec((block, columns_out), lambda i, _: (number * steps + i, 0))

    return call(
        project_kernel,
        (steps,),
        (limit,),
        [(x_block, pl.BlockSpec((block, width), lambda i, _: (i, 0)))]
        + [(array, whole_block(array)) for array in (weight, gain, shift, columns)],
        [out(GROUP_LANES), out(2 * GROUP_LANES), out(width)],
        held,
        cost=(2 * tokens * weight.size, tokens * width * 8 + weight.size * 2, tokens),
        after=after,
    )


def attend_kernel(query_ref, pair_ref, context_ref, ready_ref):
    contexts = []
    for head in range(GROUP_HEADS):
        lanes = slice(head * LANES, (head + 1) * LANES)
        queries = query_ref[:, lanes]
        scores = dot_nt(queries, pair_ref[:, lanes])
        largest = jnp.max(scores, axis=1, keepdims=True)
        exponent = jnp.exp2(scores - largest)
        values = pair_ref[:, GROUP_LANES + head * LANES : GROUP_LANES + (head + 1) * LANES]
        mixed = dot_nn(exponent.astype(LOW), values)
        summed = mixed[:, HD : HD + 1]
        contexts.append((mixed / summed)[:, :HD])
        log_parts = split_three(-(largest + jnp.log2(summed)))
        ready_ref[:, lanes] = with_lanes(queries.astype(jnp.float32), HD + 1, log_parts).astype(LOW)
    context_ref[...] = jnp.concatenate(contexts, axis=1).astype(LOW)


def attend(number, queries, pair, after=()):
    rows = queries.shape[0]
    tokens = rows // CLIP_DEV
    block = divisor(tokens, QUERY_BLOCK)
    steps = tokens // block
    spot = pl.BlockSpec((block, GROUP_LANES), lambda i: (number * steps + i, 0))
    context, ready = call(
        attend_kernel,
        (steps,),
        (),
        [(queries, spot), (pair, whole_block(pair))],
        [
            (like(tokens, GROUP_WIDTH), pl.BlockSpec((block, GROUP_WIDTH), lambda i: (i, 0))),
            (like(tokens, GROUP_LANES), pl.BlockSpec((block, GROUP_LANES), lambda i: (i, 0))),
        ],
        cost=(4 * tokens * rows * GROUP_LANES * 2, rows * GROUP_LANES * 6, tokens * rows * GROUP_HEADS),
        after=after,
    )
    return context, ready


def attend_back_kernel(
    head,
    query_ref,
    key_ref,
    value_ref,
    context_ref,
    grad_ref,
    grad_query_ref,
    grad_key_ref,
    grad_value_ref,
    key_turned,
    key_total,
    value_total,
):
    step = pl.program_id(0)

    @pl.when(step == 0)
    def _():
        key_turned[...] = key_ref[...].T
        key_total[...] = jnp.zeros_like(key_total)
        value_total[...] = jnp.zeros_like(value_total)

    lanes = slice(head * HD, (head + 1) * HD)
    queries = query_ref[...]
    grad = grad_ref[:, lanes].astype(jnp.float32)
    row_term = jnp.sum(grad * context_ref[:, lanes].astype(jnp.float32), axis=1, keepdims=True)
    grad = jnp.concatenate([grad, jnp.zeros((grad.shape[0], LANES - HD), jnp.float32)], axis=1)
    grad = with_lanes(grad, HD, split_three(-row_term)).astype(LOW)
    soft = jnp.exp2(dot_nt(key_ref[...], queries))
    grad_soft = dot_nt(value_ref[...], grad)
    value_total[...] += dot_nn(soft.astype(LOW), grad)
    grad_scores = (soft * grad_soft).astype(LOW)
    key_total[...] += dot_nn(grad_scores, queries)
    grad_query = dot_nn(key_turned[...], grad_scores)
    grad_query_ref[...] = (grad_query * HD ** (-0.5)).T.astype(LOW)

    @pl.when(step == pl.num_programs(0) - 1)
    def _():
        grad_key_ref[...] = (key_total[...] * LN2).astype(LOW)
        grad_value_ref[...] = value_total[...].astype(LOW)


def attend_back(head, queries, pair, context, grad_context, held, after=()):
    rows = queries.shape[0]
    block = divisor(rows, GRAD_BLOCK)
    part = pl.BlockSpec((block, LANES), lambda i: (i, head))
    compact = pl.BlockSpec((block, GROUP_WIDTH), lambda i: (i, 0))
    out = like(rows, GROUP_LANES)
    whole = pl.BlockSpec((rows, LANES), lambda i: (0, head))
    return call(
        functools.partial(attend_back_kernel, head),
        (rows // block,),
        (),
        [
            (queries, part),
            (pair, whole),
            (pair, pl.BlockSpec((rows, LANES), lambda i: (0, GROUP_HEADS + head))),
            (context, compact),
            (grad_context, compact),
        ],
        [(out, part), (out, whole), (out, whole)],
        held,
        scratch=[
            pltpu.VMEM((LANES, rows), LOW),
            pltpu.VMEM((rows, LANES), jnp.float32),
            pltpu.VMEM((rows, LANES), jnp.float32),
        ],
        cost=(20 * rows * rows * LANES, 10 * rows * LANES * 2, rows * rows),
        after=after,
    )


def entry_back_kernel(x_ref, query_ref, key_ref, value_ref, weight_ref, partial_ref, sums_ref):
    partial = dot_nn(query_ref[...], weight_ref[:GROUP_LANES, :])
    partial += dot_nn(key_ref[...], weight_ref[GROUP_LANES : 2 * GROUP_LANES, :])
    partial += dot_nn(value_ref[...], weight_ref[2 * GROUP_LANES :, :])
    partial_ref[...] = partial.astype(LOW)
    unit = unit_rows_of(x_ref[...].astype(jnp.float32))

    @pl.when(pl.program_id(0) == 0)
    def _():
        sums_ref[...] = jnp.zeros_like(sums_ref)

    sums_ref[0:1, :] += jnp.sum(partial * unit, axis=0, keepdims=True)
    sums_ref[1:2, :] += jnp.sum(partial, axis=0, keepdims=True)


def entry_back(number, x_block, grads, weight, after=()):
    tokens, width = x_block.shape
    block = divisor(tokens, TOKEN_BLOCK)
    steps = tokens // block
    spot = pl.BlockSpec((block, width), lambda i: (i, 0))
    return call(
        entry_back_kernel,
        (steps,),
        (),
        [(x_block, spot)]
        + [(grad, pl.BlockSpec((block, GROUP_LANES), lambda i: (number * steps + i, 0))) for grad in grads]
        + [(weight, whole_block(weight))],
        [(like(tokens, width), spot), (like(8, width, jnp.float32), pl.BlockSpec((8, width), lambda i: (0, 0)))],
        cost=(2 * tokens * weight.size, tokens * width * 8 + weight.size * 2, tokens),
        after=after,
    )


def widen_kernel(normed_ref, weight_ref, bias_ref, activated_ref, slope_ref):
    widened = dot_nt(normed_ref[...], weight_ref[...]) + bias_ref[...]
    below = 0.5 + 0.5 * lax.erf(widened * math.sqrt(0.5))
    activated_ref[...] = (widened * below).astype(LOW)
    density = jnp.exp2(widened * widened * (-0.5 * math.log2(math.e))) * (1.0 / math.sqrt(2.0 * math.pi))
    slope_ref[...] = (below + widened * density).astype(LOW)


def widen(number, normed, weight, bias, held, after=()):
    tokens, width = normed.shape
    units = weight.shape[0]
    block = divisor(units, UNIT_BLOCK)
    spot = pl.BlockSpec((tokens, block), lambda i: (number, i))
    out = like(2 * tokens, units)
    return call(
        widen_kernel,
        (units // block,),
        (),
        [
            (normed, whole_block(normed)),
            (weight, pl.BlockSpec((block, width), lambda i: (i, 0))),
            (bias.reshape(1, units), pl.BlockSpec((1, block), lambda i: (0, i))),
        ],
        [(out, spot), (out, spot)],
        held,
        cost=(2 * tokens * weight.size + 40 * tokens * units, weight.size * 2 + tokens * units * 4, 2 * tokens * units),
        after=after,
    )


def split_columns(piece, core, shards):
    rows, columns = piece.shape
    span = columns // shards // 2

    def body(core_ref, piece_ref, out_ref):
        for shard in range(shards):
            low = piece_ref[:, 2 * shard * span : (2 * shard + 1) * span]
            high = piece_ref[:, (2 * shard + 1) * span : (2 * shard + 2) * span]
            out_ref[:, shard * span : (shard + 1) * span] = jnp.where(core_ref[0] == 0, low, high)

    spec = pl.BlockSpec((rows, columns // 2), lambda *_: (0, 0))
    return call(body, (1,), (core.reshape(1),), [(piece, whole_block(piece))], [(like(rows, columns // 2), spec)])[0]


def merge_columns(mine, other, core, shards):
    rows, columns = mine.shape
    span = columns // shards

    def body(core_ref, mine_ref, other_ref, out_ref):
        for shard in range(shards):
            a = mine_ref[:, shard * span : (shard + 1) * span].astype(jnp.float32)
            b = other_ref[:, shard * span : (shard + 1) * span].astype(jnp.float32)
            first = core_ref[0] == 0
            out_ref[:, 2 * shard * span : (2 * shard + 1) * span] = jnp.where(first, a, b)
            out_ref[:, (2 * shard + 1) * span : (2 * shard + 2) * span] = jnp.where(first, b, a)

    spec = pl.BlockSpec((rows, 2 * columns), lambda *_: (0, 0))
    return call(
        body,
        (1,),
        (core.reshape(1),),
        [(mine, whole_block(mine)), (other, whole_block(other))],
        [(like(rows, 2 * columns, jnp.float32), spec)],
    )[0]


def normalise(values):
    center = values - jnp.mean(values, axis=-1, keepdims=True)
    spread = jnp.mean(center * center, axis=-1, keepdims=True)
    scale = lax.rsqrt(spread + EPSILON)
    return center * scale, scale


def norm_back(grad, gain, unit, scale):
    scaled = grad * gain
    return scale * (
        scaled
        - jnp.mean(scaled, axis=-1, keepdims=True)
        - unit * jnp.mean(scaled * unit, axis=-1, keepdims=True)
    )


def pick(blocks, index, axis=0):
    return lax.dynamic_index_in_dim(blocks, index, axis, keepdims=False)


def widen_bit(held, place, axis, mask, mine):
    came = swap(held, axis, mask)
    return jnp.where(
        mine == 1,
        jnp.concatenate([came, held], axis=place),
        jnp.concatenate([held, came], axis=place),
    )


def gather_bits(piece, bits):
    held = piece.reshape((1,) * len(bits) + piece.shape)
    for place in sorted(range(len(bits)), key=lambda i: bits[i][3]):
        axis, mask, mine, _ = bits[place]
        held = widen_bit(held, place, axis, mask, mine)
    return held


def halve(held, place, axis, mask, mine):
    kept = pick(held, mine, place)
    came = swap(pick(held, 1 - mine, place), axis, mask)
    return (kept.astype(jnp.float32) + came.astype(jnp.float32)).astype(LOW)


def gather_near(held, turn):
    blocks = held.shape[0]
    held = held.reshape(-1, held.shape[2])
    masks = [(i, 0, 0) for i in range(blocks)]
    copies = lax.axis_size("dp") // 2
    steps = [("dp", 1 << level) for level in range(copies.bit_length() - 1)]
    steps = [("fsdp", 1)] + steps if turn else steps + [("fsdp", 1)]
    parts, stages = [], []
    for number, (axis, mask) in enumerate(steps):
        came = swap(held, axis, 2 * mask if axis == "dp" else mask)
        stages.append(came)
        came_masks = [
            (far, near ^ (mask if axis == "fsdp" else 0), copy ^ (mask if axis == "dp" else 0))
            for far, near, copy in masks
        ]
        if number == len(steps) - 1:
            parts = [(held, masks), (came, came_masks)]
        else:
            held, masks = jnp.concatenate([held, came]), masks + came_masks
    return parts, stages


def assemble(low, high, shape, block_rows, axis):
    copies = lax.axis_size("dp") // 2
    near, copy = lax.axis_index("fsdp") % 2, lax.axis_index("dp") // 2
    columns = low[0][0].shape[1]

    def target(mask):
        return ((2 * mask[0] + (near ^ mask[1])) * copies + (copy ^ mask[2])).astype(jnp.int32)

    order = [mask for _, masks in low for mask in masks]
    out_rows = shape[0] // len(order)
    if block_rows % 16:
        out = jnp.zeros(shape, LOW)
        for offset, parts in ((0, low), (1, high)):
            for array, masks in parts:
                for number, mask in enumerate(masks):
                    block = array[number * block_rows : (number + 1) * block_rows]
                    start = target(mask) * out_rows
                    shift = (0, offset * columns) if axis else (offset * block_rows, 0)
                    out = lax.dynamic_update_slice(out, block, (start + shift[0], shift[1]))
        return out

    sources = low + high
    tables, uses = [], []
    for _, masks in sources:
        at, table = 0, []
        for mask in order:
            at = masks.index(mask) if mask in masks else at
            table.append(at)
        tables.append(table)
        uses.append([int(mask in masks) for mask in order])
    steps = len(order)
    flat = [target(mask) for mask in order]
    fixed = jnp.array([x for table in tables + uses for x in table], jnp.int32)
    scalars = jnp.concatenate([jnp.stack(flat), fixed])

    def body(table_ref, *refs):
        step = pl.program_id(0)
        out_ref = refs[-1]
        for part, source in enumerate(refs[:-1]):
            first = part < len(low)
            if axis:
                spot = (slice(None), slice(0, columns) if first else slice(columns, 2 * columns))
            else:
                spot = (slice(0, block_rows) if first else slice(block_rows, 2 * block_rows), slice(None))

            @pl.when(table_ref[steps * (1 + len(sources) + part) + step] == 1)
            def _(source=source, spot=spot):
                out_ref[spot] = source[...]

    def source_spec(part):
        return pl.BlockSpec((block_rows, columns), lambda i, t: (t[steps * (1 + part) + i], 0))

    out_block = (block_rows, 2 * columns) if axis else (2 * block_rows, columns)
    return call(
        body,
        (steps,),
        (scalars,),
        [(array, source_spec(part)) for part, (array, _) in enumerate(sources)],
        [(like(*shape), pl.BlockSpec(out_block, lambda i, t: (t[i], 0)))],
        cost=(0, 4 * shape[0] * shape[1], 0),
    )[0]


def zero_after(*arrays):
    zero = jnp.int32(0)
    for array in arrays:
        first = array[(0,) * array.ndim].astype(jnp.float32)
        zero += (jnp.abs(first) * 2.0 < -1.0).astype(jnp.int32)
    return zero


def on_device(
    hidden_states,
    clip_lengths,
    norm_gains,
    norm_shifts,
    proj_biases,
    up_bias,
    in_proj,
    out_proj,
    up_proj,
    down_proj,
    cotangent,
):
    tokens_here, width = hidden_states.shape
    fsdp_count = lax.axis_size("fsdp")
    dp_count = lax.axis_size("dp")
    fsdp_index = lax.axis_index("fsdp")
    dp_index = lax.axis_index("dp")
    core = dp_index % 2
    copies = dp_count // 2
    copy_index = dp_index // 2
    region = (dp_index * fsdp_count + fsdp_index) // CLIP_DEV
    place = fsdp_index % CLIP_DEV
    length = lax.dynamic_index_in_dim(clip_lengths, region, keepdims=False)
    span = tokens_here * CLIP_DEV
    hidden_units = up_bias.shape[0]
    positions = jnp.arange(tokens_here, dtype=jnp.int32)
    row_valid = (place * tokens_here + positions < length).astype(jnp.float32)
    copy_levels = copies.bit_length() - 1
    fsdp_levels = fsdp_count.bit_length() - 1
    far_count = fsdp_count // 2
    half = width // 2

    core_bit = ("dp", 1, core, 1000)
    copy_bits = [("dp", 2 << level, copy_index >> level & 1, 200 - level) for level in reversed(range(copy_levels))]
    fsdp_bits = [
        ("fsdp", 1 << level, fsdp_index >> level & 1, fsdp_count - level)
        for level in reversed(range(fsdp_levels))
    ]

    with jax.named_scope("gather_tokens"):
        near = swap(hidden_states, "fsdp", 1)
        far = swap(hidden_states, "fsdp", 2)
        both = jnp.concatenate([swap(near[:, :half], "fsdp", 2), swap(far[:, half:], "fsdp", 1)], axis=1)
        clip_blocks = [hidden_states, near, far, both]

    with jax.named_scope("gather_in_proj"):
        rounds = fsdp_count // CLIP_DEV
        unit_rows = in_proj.shape[0] // 3
        piece_rows = unit_rows // dp_count
        own_units = in_proj.reshape(3, 2, copies, piece_rows, width)
        own_units = pick(pick(own_units, core, 1), copy_index, 1)

        def route(slot, turn):
            pairs = []
            for source in range(fsdp_count):
                unit = (3 * source + slot) % fsdp_count
                owner, spot = unit // rounds, unit % rounds
                pairs.append((source, owner + CLIP_DEV * ((spot + turn) % rounds)))
            return pairs

        entry_bits = [core_bit] + copy_bits
        came = jnp.stack(
            [
                jnp.stack([lax.ppermute(own_units[slot], "fsdp", route(slot, turn)) for turn in range(rounds)])
                for slot in range(3)
            ]
        )
        came = gather_bits(came, entry_bits)
        came = came.reshape(dp_count, 3, rounds, piece_rows, width)
        came = jnp.moveaxis(came, 0, 2).reshape(3, rounds, unit_rows, width)
        lap = fsdp_index // CLIP_DEV

        def slot_of(kind, spot):
            return (place * rounds + spot + kind * fsdp_count) % 3

        weight_rows = jnp.stack(
            [
                jnp.concatenate(
                    [
                        pick(pick(came, slot_of(kind, spot)), (lap - spot) % rounds)
                        for spot in range(rounds)
                    ]
                )
                for kind in range(3)
            ]
        )
        padded_width = 3 * GROUP_LANES
        weight_in = jnp.pad(
            weight_rows.reshape(3 * GROUP_HEADS, HD, width), ((0, 0), (0, LANES - HD), (0, 0))
        ).reshape(padded_width, width)

    zeros = jnp.zeros((width,), jnp.float32)
    group_bias = jnp.stack([proj_biases[0] * SCORE_SCALE, zeros, proj_biases[1]])
    group_bias = pick(group_bias.reshape(3, CLIP_DEV, GROUP_HEADS, HD), place, 1)
    group_bias = jnp.pad(group_bias, ((0, 0), (0, 0), (0, LANES - HD)))
    lane = jnp.arange(LANES)
    spare = jnp.stack(
        [
            lane == HD,
            (lane > HD) & (lane <= HD + 3),
            (lane >= HD) & (lane < HD + 3),
        ]
    ).astype(jnp.float32)
    columns = (group_bias + spare[:, None]).reshape(1, padded_width)
    held = None
    for number in range(CLIP_DEV):
        limit = (length - (place ^ number) * tokens_here).reshape(1)
        held = project(
            number, clip_blocks[number], weight_in, norm_gains[0:1], norm_shifts[0:1], columns, limit, held
        )
    queries, pair, normed_one = held

    with jax.named_scope("gather_up_and_out_proj"):
        out_rows = out_proj.shape[0] // dp_count
        shard_units = up_proj.shape[0]
        half_units = shard_units // 2
        up_rows = half_units // copies
        up_part = up_rows // 2
        zero = zero_after(near, far, came)
        out_piece = pick(pick(out_proj.reshape(copies, 2, out_rows, width), copy_index + zero), core)
        up_piece = pick(pick(up_proj.reshape(2, copies, up_rows, width), core + zero), copy_index)
        up_far = gather_bits(jnp.concatenate([up_piece, out_piece]), fsdp_bits[:-1])
        up_far = up_far.reshape(far_count, up_rows + out_rows, width)
    with jax.named_scope("gather_out_proj"):
        out_full = up_far[:, up_rows:].reshape((far_count, 1) + (1,) * copy_levels + (1, out_rows, width))
        out_stages = []
        for number, bit in enumerate([fsdp_bits[-1]] + copy_bits + [core_bit]):
            out_full = widen_bit(out_full, number + 1, *bit[:3])
            out_stages.append(out_full)
        out_full = out_full.reshape(width, width)
    with jax.named_scope("gather_up_proj"):
        low, low_stages = gather_near(up_far[:, :up_part], True)
        high, high_stages = gather_near(up_far[:, up_part:up_rows], False)
        up_stages = [low_stages, high_stages]
        up_half = assemble(low, high, (hidden_units // 2, width), up_part, 0)
    with jax.named_scope("gather_down_proj"):
        down_rows = down_proj.shape[0] // copies
        quarter = hidden_units // 4
        down_piece = pick(down_proj.reshape(copies, down_rows, hidden_units), copy_index + zero_after(up_far))
        down_piece = split_columns(down_piece, core, fsdp_count)
        down_piece = jnp.concatenate([down_piece[:, :quarter], down_piece[:, quarter:]])
        down_far = gather_bits(down_piece, fsdp_bits[:-1]).reshape(far_count, 2 * down_rows, quarter)
        low, low_stages = gather_near(down_far[:, :down_rows], True)
        high, high_stages = gather_near(down_far[:, down_rows:], False)
        down_half = assemble(low, high, (width, hidden_units // 2), down_rows, 1)

    contexts, ready = [None] * CLIP_DEV, [None] * CLIP_DEV
    gates = [[up_far], out_stages[:1], [up_stages[0][0], up_stages[1][0], out_stages[1]], [down_far, out_stages[-1]]]
    for number, gate in zip((3, 1, 2, 0), gates, strict=True):
        contexts[number], ready[number] = attend(number, queries, pair, gate)
    with jax.named_scope("context_back"):
        parts = [contexts[0]] + [swap(contexts[j], "fsdp", j) for j in range(1, CLIP_DEV)]
        parts = jnp.stack(parts)
        context_low = jnp.concatenate([pick(parts, place ^ group) for group in range(CLIP_DEV)], axis=1)
    context_heads = jnp.concatenate(contexts)
    queries_ready = jnp.concatenate(ready)

    inputs = hidden_states.astype(jnp.float32)
    grad_other = swap(cotangent, "dp", 1)
    grad_pair = jnp.concatenate([cotangent, grad_other])
    attention = dot_nt(context_low, out_full) + proj_biases[2]
    middle = inputs + attention
    unit_two, scale_two = normalise(middle)
    normed_two = (unit_two * norm_gains[1] + norm_shifts[1]).astype(LOW)
    normed_other = swap(normed_two, "dp", 1)
    half_bias = pick(up_bias.reshape(fsdp_count, 2, half_units), core, 1).reshape(hidden_units // 2)
    held = widen(0, normed_two, up_half, half_bias, None)
    activated, slope = widen(1, normed_other, up_half, half_bias, held)
    normed_pair = jnp.concatenate([normed_two, normed_other])
    grad_activated = dot_nn(grad_pair, down_half)
    grad_widened = (grad_activated * slope.astype(jnp.float32)).astype(LOW)

    def over_cores(rows, product):
        sent = product(rows[tokens_here:]).astype(LOW)
        return product(rows[:tokens_here]) + swap(sent, "dp", 1).astype(jnp.float32)

    grad_normed_two = over_cores(grad_widened, lambda rows: dot_nn(rows, up_half))
    feedforward = over_cores(activated, lambda rows: dot_nt(rows, down_half)) + proj_biases[3]
    outputs = (middle + feedforward).astype(LOW)
    stat_terms = jnp.stack(
        [
            jnp.sum(row_valid * jnp.sum(middle * middle, axis=1)),
            jnp.sum(row_valid * jnp.sum(attention * attention, axis=1)),
            jnp.sum(row_valid * jnp.sum(feedforward * feedforward, axis=1)),
        ]
    )
    grad_out = cotangent.astype(jnp.float32)
    grad_middle = grad_out + norm_back(grad_normed_two, norm_gains[1], unit_two, scale_two)
    grad_attention = grad_middle.astype(LOW)
    grad_context = dot_nn(grad_attention, out_full).astype(LOW)

    with jax.named_scope("grad_context_to_heads"):
        groups = [grad_context[:, i * GROUP_WIDTH : (i + 1) * GROUP_WIDTH] for i in range(CLIP_DEV)]
        groups = jnp.stack(groups)
        sends = [pick(groups, place ^ j) for j in range(CLIP_DEV)]
        grad_heads = jnp.concatenate([sends[0]] + [swap(sends[j], "fsdp", j) for j in range(1, CLIP_DEV)])

    grad_down = dot_tn(grad_pair, activated).astype(LOW)
    grad_up = dot_tn(grad_widened, normed_pair).astype(LOW)
    grad_exit = dot_tn(grad_attention, context_low).astype(LOW)

    def reduce_copies(grad, axis):
        grad = grad.reshape(grad.shape[:axis] + (2,) * copy_levels + grad.shape[axis + 1 :])
        for level in reversed(range(copy_levels)):
            grad = halve(grad, axis, "dp", 2 << level, copy_index >> level & 1)
        return grad

    def reduce_near(grad, turn):
        if turn:
            first = reduce_copies(grad, 2)
            return halve(first, 1, "fsdp", 1, fsdp_index % 2), first
        first = halve(grad, 1, "fsdp", 1, fsdp_index % 2)
        return reduce_copies(first, 1), first

    def reduce_far(grad):
        stages = []
        grad = grad.reshape((2,) * (fsdp_levels - 1) + grad.shape[1:])
        for axis, mask, mine, _ in fsdp_bits[:-1]:
            grad = halve(grad, 0, axis, mask, mine)
            stages.append(grad)
        return grad, stages

    with jax.named_scope("reduce_down_proj"):
        grad = grad_down.reshape(far_count, 2, copies, down_rows, hidden_units // 2)
        low_half, low_first = reduce_near(grad[..., :quarter], True)
        high_half, high_first = reduce_near(grad[..., quarter:], False)
        down_first = [low_first, high_first]
        down_second = jnp.concatenate([low_half, high_half], axis=1)
        down_sum, down_stages = reduce_far(down_second)
        down_sum = jnp.concatenate([down_sum[:down_rows], down_sum[down_rows:]], axis=1)
        down_sum = gather_bits(down_sum, copy_bits).reshape(down_rows * copies, hidden_units // 2)
        down_sum = merge_columns(down_sum, swap(down_sum, "dp", 1), core, fsdp_count)
    with jax.named_scope("reduce_up_proj"):
        grad = grad_up.reshape(far_count, 2, copies, 2, up_part, width)
        low_half, low_first = reduce_near(grad[:, :, :, 0], True)
        high_half, high_first = reduce_near(grad[:, :, :, 1], False)
        up_first = [low_first, high_first]
        exit_core = halve(grad_exit.reshape(far_count, 2, copies, 2, out_rows, width), 3, "dp", 1, core)
        exit_grad, exit_first = reduce_near(exit_core, True)
        up_second = jnp.concatenate([low_half, high_half, exit_grad], axis=1)
        sums, far_stages = reduce_far(up_second)
        sums = gather_bits(sums, [core_bit] + copy_bits).reshape(2, copies, up_rows + out_rows, width)
        up_sum = sums[:, :, :up_rows].reshape(up_proj.shape).astype(jnp.float32)
        exit_sum = jnp.moveaxis(sums[:, :, up_rows:], 0, 1).reshape(out_proj.shape).astype(jnp.float32)

    held = None
    gates = [[], down_first, up_first + [exit_core], [down_second, exit_first]]
    for head in range(GROUP_HEADS):
        held = attend_back(head, queries_ready, pair, context_heads, grad_heads, held, gates[head])
    grad_query, grad_key, grad_value = held
    kinds = (grad_query, grad_key, grad_value)

    with jax.named_scope("reduce_tokens"):
        partial = [None] * CLIP_DEV
        entry_sums = 0.0
        gates = {3: [up_second], 1: [], 2: [down_stages[0]], 0: []}
        for number in (3, 1, 2, 0):
            partial[number], sums = entry_back(number, clip_blocks[number], kinds, weight_in, gates[number])
            entry_sums += sums[:2]
        came_a = swap(partial[3][:, :half], "fsdp", 2)
        came_b = swap(partial[3][:, half:], "fsdp", 1)
        near_sum = jnp.concatenate(
            [
                (partial[1][:, :half].astype(jnp.float32) + came_a.astype(jnp.float32)).astype(LOW),
                partial[1][:, half:],
            ],
            axis=1,
        )
        far_sum = jnp.concatenate(
            [
                partial[2][:, :half],
                (partial[2][:, half:].astype(jnp.float32) + came_b.astype(jnp.float32)).astype(LOW),
            ],
            axis=1,
        )
        grad_normed_one = partial[0].astype(jnp.float32)
        grad_normed_one += swap(near_sum, "fsdp", 1).astype(jnp.float32)
        grad_normed_one += swap(far_sum, "fsdp", 2).astype(jnp.float32)

    with jax.named_scope("reduce_in_proj"):
        entry = jnp.stack([dot_tn(grad, normed_one).astype(LOW) for grad in kinds])
        entry = entry.reshape(3, GROUP_HEADS, LANES, width)[:, :, :HD]
        entry = entry.reshape(3, rounds, 2, copies, piece_rows, width)
        entry = halve(entry, 2, "dp", 1, core)
        entry = reduce_copies(entry, 2)
        totals = []
        for slot in range(3):
            total = 0.0
            for turn in range(rounds):
                spot = (lap - turn) % rounds
                kind = ((slot - place * rounds - spot) * pow(fsdp_count, -1, 3)) % 3
                sent = pick(pick(entry, kind), spot)
                back = [(target, source) for source, target in route(slot, turn)]
                total = total + lax.ppermute(sent, "fsdp", back).astype(jnp.float32)
            totals.append(total.astype(LOW))
        entry_sum = gather_bits(jnp.stack(totals), entry_bits)
        entry_sum = entry_sum.reshape(dp_count, 3, piece_rows, width)
        entry_sum = jnp.moveaxis(entry_sum, 1, 0).reshape(in_proj.shape).astype(jnp.float32)

    unit_one, scale_one = normalise(inputs)
    grad_hidden = grad_middle + norm_back(grad_normed_one, norm_gains[0], unit_one, scale_one)

    def place_heads(grads):
        sums = jnp.sum(grads.astype(jnp.float32), axis=0).reshape(GROUP_HEADS, LANES)[:, :HD]
        rows = jnp.zeros((CLIP_DEV, GROUP_WIDTH), jnp.float32)
        return lax.dynamic_update_index_in_dim(rows, sums.reshape(GROUP_WIDTH), place, 0).reshape(width)

    with jax.named_scope("small_sums"):
        half_up = jnp.sum(grad_widened.astype(jnp.float32), axis=0).reshape(fsdp_count, half_units)
        up_terms = jnp.zeros((fsdp_count, 2, half_units), jnp.float32)
        up_terms = lax.dynamic_update_index_in_dim(up_terms, half_up, core, 1).reshape(hidden_units // width, width)
        small = jnp.concatenate(
            [
                jnp.stack(
                    [
                        jnp.sum(grad_normed_two * unit_two, axis=0),
                        jnp.sum(grad_normed_two, axis=0),
                        place_heads(grad_query),
                        place_heads(grad_value),
                        jnp.sum(grad_attention.astype(jnp.float32), axis=0),
                        jnp.sum(grad_out, axis=0),
                        jnp.pad(stat_terms, (0, width - 3)),
                    ]
                ),
                up_terms,
                entry_sums,
            ]
        )
        for axis in ("dp", "fsdp"):
            for level in range(lax.axis_size(axis).bit_length() - 1):
                small = small + swap(small, axis, 1 << level)
    valid_count = jnp.sum(clip_lengths).astype(jnp.float32) * width
    root_means = jnp.sqrt(small[6, :3] / valid_count)
    return (
        outputs,
        grad_hidden.astype(LOW),
        entry_sum,
        exit_sum,
        up_sum,
        down_sum,
        jnp.stack([small[-2], small[0]]),
        jnp.stack([small[-1], small[1]]),
        small[2:6],
        small[7:-2].reshape(hidden_units),
        root_means,
    )


def solution(mesh):
    in_specs = (
        P(("dp", "fsdp"), None),
        P(),
        P(),
        P(),
        P(),
        P(),
        P("fsdp", None),
        P("fsdp", None),
        P("fsdp", None),
        P("fsdp", None),
        P(("dp", "fsdp"), None),
    )
    out_specs = (
        P(("dp", "fsdp"), None),
        P(("dp", "fsdp"), None),
        P("fsdp", None),
        P("fsdp", None),
        P("fsdp", None),
        P("fsdp", None),
        P(),
        P(),
        P(),
        P(),
        P(),
    )
    return jax.shard_map(
        on_device, mesh=mesh, in_specs=in_specs, out_specs=out_specs, check_vma=False
    )
```

```python
import functools
import math

import jax
import jax.numpy as jnp
from jax import lax
from jax.experimental import pallas as pl
from jax.experimental.pallas import tpu as pltpu
from jax.sharding import PartitionSpec as P

H = 16
HD = 80
CLIP_DEV = 4
LANES = 128
GROUP_HEADS = H // CLIP_DEV
EPSILON = 1e-05
SCORE_SCALE = HD ** (-0.5) * math.log2(math.e)
LN2 = math.log(2.0)
LOW = jnp.bfloat16
TOKEN_BLOCK = 256
QUERY_BLOCK = 512
GRAD_BLOCK = 512
UNIT_BLOCK = 1280
GROUP_LANES = GROUP_HEADS * LANES
GROUP_WIDTH = GROUP_HEADS * HD
VMEM_BYTES = 56 * 1024 * 1024


def swap(value, axis, mask):
    pairs = [(source, source ^ mask) for source in range(lax.axis_size(axis))]
    return lax.ppermute(value, axis, pairs)


def swap_by_core(value, first, second):
    fsdp = lax.axis_size("fsdp")
    pairs = []
    for dp in range(lax.axis_size("dp")):
        axis, mask = second if dp % 2 else first
        for index in range(fsdp):
            target = (dp ^ mask) * fsdp + index if axis == "dp" else dp * fsdp + (index ^ mask)
            pairs.append((dp * fsdp + index, target))
    return lax.ppermute(value, ("dp", "fsdp"), pairs)


def dot_nt(lhs, rhs):
    return lax.dot_general(
        lhs, rhs, (((1,), (1,)), ((), ())), preferred_element_type=jnp.float32
    )


def dot_nn(lhs, rhs):
    return jnp.dot(lhs, rhs, preferred_element_type=jnp.float32)


def dot_tn(lhs, rhs):
    return lax.dot_general(
        lhs, rhs, (((0,), (0,)), ((), ())), preferred_element_type=jnp.float32
    )


def split_three(value):
    high = value.astype(LOW).astype(jnp.float32)
    rest = value - high
    middle = rest.astype(LOW).astype(jnp.float32)
    return high, middle, rest - middle


def with_lanes(block, first, columns):
    lane = lax.broadcasted_iota(jnp.int32, block.shape, 1)
    for place, column in enumerate(columns):
        block = jnp.where(lane == first + place, column, block)
    return block


def divisor(size, most):
    block = min(size, most)
    while size % block:
        block //= 2
    return block


ANYWHERE = pl.BlockSpec(memory_space=pl.ANY)


def call(body, grid, scalars, inputs, outputs, held=None, scratch=(), cost=(0, 0, 0), after=()):
    held = () if held is None else tuple(held)
    passive = held + tuple(after)
    n_scalar, n_in, n_passive, n_out = len(scalars), len(inputs), len(passive), len(outputs)

    def kernel(*refs):
        first = n_scalar + n_in
        body(*refs[:first], *refs[first + n_passive :])

    flops, moved, special = cost
    return pl.pallas_call(
        kernel,
        grid_spec=pltpu.PrefetchScalarGridSpec(
            num_scalar_prefetch=n_scalar,
            grid=grid,
            in_specs=[spec for _, spec in inputs] + [ANYWHERE] * n_passive,
            out_specs=[spec for _, spec in outputs],
            scratch_shapes=list(scratch),
        ),
        out_shape=[shape for shape, _ in outputs],
        input_output_aliases={n_scalar + n_in + i: i for i in range(len(held))},
        compiler_params=pltpu.CompilerParams(vmem_limit_bytes=VMEM_BYTES),
        cost_estimate=pl.CostEstimate(flops=int(flops), bytes_accessed=int(moved), transcendentals=int(special)),
    )(*scalars, *(array for array, _ in inputs), *passive)


def like(rows, columns, kind=LOW):
    return jax.ShapeDtypeStruct((rows, columns), kind)


def whole_block(array):
    return pl.BlockSpec(array.shape, lambda *_: (0,) * len(array.shape))


def fence(token, reads, *arrays):
    def body(*refs):
        pass

    carried = (token, *arrays)
    return pl.pallas_call(
        body,
        in_specs=[ANYWHERE] * (len(carried) + len(reads)),
        out_specs=[ANYWHERE] * len(carried),
        out_shape=[jax.ShapeDtypeStruct(array.shape, array.dtype) for array in carried],
        input_output_aliases={i: i for i in range(len(carried))},
        cost_estimate=pl.CostEstimate(flops=0, bytes_accessed=0, transcendentals=0),
    )(*carried, *reads)


def unit_rows_of(values):
    center = values - jnp.mean(values, axis=-1, keepdims=True)
    spread = jnp.mean(center * center, axis=-1, keepdims=True)
    return center * lax.rsqrt(spread + EPSILON)


def project_kernel(limit_ref, x_ref, weight_ref, gain_ref, shift_ref, column_ref, query_ref, pair_ref, normed_ref):
    rows = x_ref.shape[0]
    unit = unit_rows_of(x_ref[...].astype(jnp.float32))
    normed = (unit * gain_ref[...] + shift_ref[...]).astype(LOW)
    normed_ref[...] = normed
    columns = column_ref[...]
    queries = dot_nt(normed, weight_ref[:GROUP_LANES, :])
    query_ref[...] = (queries * SCORE_SCALE + columns[:, :GROUP_LANES]).astype(LOW)
    pair = dot_nt(normed, weight_ref[GROUP_LANES:, :]) + columns[:, GROUP_LANES:]
    row = pl.program_id(0) * rows + lax.broadcasted_iota(jnp.int32, pair.shape, 0)
    lane = lax.broadcasted_iota(jnp.int32, pair.shape, 1)
    masked = (row >= limit_ref[0]) & (lane % LANES == HD) & (lane < GROUP_LANES)
    pair_ref[...] = jnp.where(masked, -1e30, pair).astype(LOW)


def project(number, x_block, weight, gain, shift, columns, limit, held, after=()):
    tokens, width = x_block.shape
    block = divisor(tokens, TOKEN_BLOCK)
    steps = tokens // block
    rows = CLIP_DEV * tokens

    def out(columns_out):
        return like(rows, columns_out), pl.BlockSpec((block, columns_out), lambda i, _: (number * steps + i, 0))

    return call(
        project_kernel,
        (steps,),
        (limit,),
        [(x_block, pl.BlockSpec((block, width), lambda i, _: (i, 0)))]
        + [(array, whole_block(array)) for array in (weight, gain, shift, columns)],
        [out(GROUP_LANES), out(2 * GROUP_LANES), out(width)],
        held,
        cost=(0, 0, 0),
        after=after,
    )


def attend_kernel(query_ref, pair_ref, context_ref, ready_ref):
    contexts = []
    for head in range(GROUP_HEADS):
        lanes = slice(head * LANES, (head + 1) * LANES)
        queries = query_ref[:, lanes]
        scores = dot_nt(queries, pair_ref[:, lanes])
        largest = jnp.max(scores, axis=1, keepdims=True)
        exponent = jnp.exp2(scores - largest)
        values = pair_ref[:, GROUP_LANES + head * LANES : GROUP_LANES + (head + 1) * LANES]
        mixed = dot_nn(exponent.astype(LOW), values)
        summed = mixed[:, HD : HD + 1]
        contexts.append((mixed / summed)[:, :HD])
        log_parts = split_three(-(largest + jnp.log2(summed)))
        ready_ref[:, lanes] = with_lanes(queries.astype(jnp.float32), HD + 1, log_parts).astype(LOW)
    context_ref[...] = jnp.concatenate(contexts, axis=1).astype(LOW)


def attend(number, queries, pair, after=()):
    rows = queries.shape[0]
    tokens = rows // CLIP_DEV
    block = divisor(tokens, QUERY_BLOCK)
    steps = tokens // block
    spot = pl.BlockSpec((block, GROUP_LANES), lambda i: (number * steps + i, 0))
    context, ready = call(
        attend_kernel,
        (steps,),
        (),
        [(queries, spot), (pair, whole_block(pair))],
        [
            (like(tokens, GROUP_WIDTH), pl.BlockSpec((block, GROUP_WIDTH), lambda i: (i, 0))),
            (like(tokens, GROUP_LANES), pl.BlockSpec((block, GROUP_LANES), lambda i: (i, 0))),
        ],
        cost=(0, 0, 0),
        after=after,
    )
    return context, ready


def attend_back_kernel(
    head,
    query_ref,
    key_ref,
    value_ref,
    context_ref,
    grad_ref,
    grad_query_ref,
    grad_key_ref,
    grad_value_ref,
    key_turned,
    key_total,
    value_total,
):
    step = pl.program_id(0)

    @pl.when(step == 0)
    def _():
        key_turned[...] = key_ref[...].T
        key_total[...] = jnp.zeros_like(key_total)
        value_total[...] = jnp.zeros_like(value_total)

    lanes = slice(head * HD, (head + 1) * HD)
    queries = query_ref[...]
    grad = grad_ref[:, lanes].astype(jnp.float32)
    row_term = jnp.sum(grad * context_ref[:, lanes].astype(jnp.float32), axis=1, keepdims=True)
    grad = jnp.concatenate([grad, jnp.zeros((grad.shape[0], LANES - HD), jnp.float32)], axis=1)
    grad = with_lanes(grad, HD, split_three(-row_term)).astype(LOW)
    soft = jnp.exp2(dot_nt(key_ref[...], queries))
    grad_soft = dot_nt(value_ref[...], grad)
    value_total[...] += dot_nn(soft.astype(LOW), grad)
    grad_scores = (soft * grad_soft).astype(LOW)
    key_total[...] += dot_nn(grad_scores, queries)
    grad_query = dot_nn(key_turned[...], grad_scores)
    grad_query_ref[...] = (grad_query * HD ** (-0.5)).T.astype(LOW)

    @pl.when(step == pl.num_programs(0) - 1)
    def _():
        grad_key_ref[...] = (key_total[...] * LN2).astype(LOW)
        grad_value_ref[...] = value_total[...].astype(LOW)


def attend_back(head, queries, pair, context, grad_context, held, after=()):
    rows = queries.shape[0]
    block = divisor(rows, GRAD_BLOCK)
    part = pl.BlockSpec((block, LANES), lambda i: (i, head))
    compact = pl.BlockSpec((block, GROUP_WIDTH), lambda i: (i, 0))
    out = like(rows, GROUP_LANES)
    whole = pl.BlockSpec((rows, LANES), lambda i: (0, head))
    return call(
        functools.partial(attend_back_kernel, head),
        (rows // block,),
        (),
        [
            (queries, part),
            (pair, whole),
            (pair, pl.BlockSpec((rows, LANES), lambda i: (0, GROUP_HEADS + head))),
            (context, compact),
            (grad_context, compact),
        ],
        [(out, part), (out, whole), (out, whole)],
        held,
        scratch=[
            pltpu.VMEM((LANES, rows), LOW),
            pltpu.VMEM((rows, LANES), jnp.float32),
            pltpu.VMEM((rows, LANES), jnp.float32),
        ],
        cost=(0, 0, 0),
        after=after,
    )


def entry_back_kernel(x_ref, query_ref, key_ref, value_ref, weight_ref, partial_ref, sums_ref):
    partial = dot_nn(query_ref[...], weight_ref[:GROUP_LANES, :])
    partial += dot_nn(key_ref[...], weight_ref[GROUP_LANES : 2 * GROUP_LANES, :])
    partial += dot_nn(value_ref[...], weight_ref[2 * GROUP_LANES :, :])
    partial_ref[...] = partial.astype(LOW)
    unit = unit_rows_of(x_ref[...].astype(jnp.float32))

    @pl.when(pl.program_id(0) == 0)
    def _():
        sums_ref[...] = jnp.zeros_like(sums_ref)

    sums_ref[0:1, :] += jnp.sum(partial * unit, axis=0, keepdims=True)
    sums_ref[1:2, :] += jnp.sum(partial, axis=0, keepdims=True)


def entry_back(number, x_block, grads, weight, after=()):
    tokens, width = x_block.shape
    block = divisor(tokens, TOKEN_BLOCK)
    steps = tokens // block
    spot = pl.BlockSpec((block, width), lambda i: (i, 0))
    return call(
        entry_back_kernel,
        (steps,),
        (),
        [(x_block, spot)]
        + [(grad, pl.BlockSpec((block, GROUP_LANES), lambda i: (number * steps + i, 0))) for grad in grads]
        + [(weight, whole_block(weight))],
        [(like(tokens, width), spot), (like(8, width, jnp.float32), pl.BlockSpec((8, width), lambda i: (0, 0)))],
        cost=(2 * tokens * weight.size, tokens * width * 8 + weight.size * 2, tokens),
        after=after,
    )


def widen_kernel(normed_ref, weight_ref, bias_ref, activated_ref, slope_ref):
    widened = dot_nt(normed_ref[...], weight_ref[...]) + bias_ref[...]
    below = 0.5 + 0.5 * lax.erf(widened * math.sqrt(0.5))
    activated_ref[...] = (widened * below).astype(LOW)
    density = jnp.exp2(widened * widened * (-0.5 * math.log2(math.e))) * (1.0 / math.sqrt(2.0 * math.pi))
    slope_ref[...] = (below + widened * density).astype(LOW)


def widen(number, normed, weight, bias, held, after=()):
    tokens, width = normed.shape
    units = weight.shape[0]
    block = divisor(units, UNIT_BLOCK)
    spot = pl.BlockSpec((tokens, block), lambda i: (number, i))
    out = like(2 * tokens, units)
    return call(
        widen_kernel,
        (units // block,),
        (),
        [
            (normed, whole_block(normed)),
            (weight, pl.BlockSpec((block, width), lambda i: (i, 0))),
            (bias.reshape(1, units), pl.BlockSpec((1, block), lambda i: (0, i))),
        ],
        [(out, spot), (out, spot)],
        held,
        cost=(0, 0, 0),
        after=after,
    )


def split_columns(piece, core, shards):
    rows, columns = piece.shape
    span = columns // shards // 2

    def body(core_ref, piece_ref, out_ref):
        for shard in range(shards):
            low = piece_ref[:, 2 * shard * span : (2 * shard + 1) * span]
            high = piece_ref[:, (2 * shard + 1) * span : (2 * shard + 2) * span]
            out_ref[:, shard * span : (shard + 1) * span] = jnp.where(core_ref[0] == 0, low, high)

    spec = pl.BlockSpec((rows, columns // 2), lambda *_: (0, 0))
    return call(body, (1,), (core.reshape(1),), [(piece, whole_block(piece))], [(like(rows, columns // 2), spec)])[0]


def merge_columns(mine, other, core, shards):
    rows, columns = mine.shape
    span = columns // shards

    def body(core_ref, mine_ref, other_ref, out_ref):
        for shard in range(shards):
            a = mine_ref[:, shard * span : (shard + 1) * span].astype(jnp.float32)
            b = other_ref[:, shard * span : (shard + 1) * span].astype(jnp.float32)
            first = core_ref[0] == 0
            out_ref[:, 2 * shard * span : (2 * shard + 1) * span] = jnp.where(first, a, b)
            out_ref[:, (2 * shard + 1) * span : (2 * shard + 2) * span] = jnp.where(first, b, a)

    spec = pl.BlockSpec((rows, 2 * columns), lambda *_: (0, 0))
    return call(
        body,
        (1,),
        (core.reshape(1),),
        [(mine, whole_block(mine)), (other, whole_block(other))],
        [(like(rows, 2 * columns, jnp.float32), spec)],
    )[0]


def normalise(values):
    center = values - jnp.mean(values, axis=-1, keepdims=True)
    spread = jnp.mean(center * center, axis=-1, keepdims=True)
    scale = lax.rsqrt(spread + EPSILON)
    return center * scale, scale


def norm_back(grad, gain, unit, scale):
    scaled = grad * gain
    return scale * (
        scaled
        - jnp.mean(scaled, axis=-1, keepdims=True)
        - unit * jnp.mean(scaled * unit, axis=-1, keepdims=True)
    )


def pick(blocks, index, axis=0):
    return lax.dynamic_index_in_dim(blocks, index, axis, keepdims=False)


def join_bit(held, came, place, mine):
    return jnp.where(
        mine == 1,
        jnp.concatenate([came, held], axis=place),
        jnp.concatenate([held, came], axis=place),
    )


def widen_bits(held, bits, first):
    for number, (axis, mask, mine) in enumerate(bits):
        held = join_bit(held, swap(held, axis, mask), first + number, mine)
    return held


def give(held, place, bit):
    axis, mask, mine = bit
    return swap(pick(held, 1 - mine, place), axis, mask)


def keep(held, came, place, bit):
    kept = pick(held, bit[2], place)
    return (kept.astype(jnp.float32) + came.astype(jnp.float32)).astype(LOW)


def reduce_bits(held, bits, place):
    for bit in bits:
        held = keep(held, give(held, place, bit), place, bit)
    return held


def reduce_last(held, bits):
    for place in reversed(range(len(bits))):
        held = keep(held, give(held, place, bits[place]), place, bits[place])
    return held


def gather_blocks(array, index):
    count = index.shape[0]

    def body(index_ref, source_ref, out_ref):
        for number in range(count):
            out_ref[number] = source_ref[index_ref[number]]

    shape = jax.ShapeDtypeStruct((count,) + array.shape[1:], array.dtype)
    return call(
        body,
        (1,),
        (index,),
        [(array, whole_block(array))],
        [(shape, whole_block(shape))],
        cost=(0, 0, 0),
    )[0]


def spread_heads(mine, other, core, index, rounds):
    copies, _, rows, width = mine.shape
    if rows % 8:
        blocks = jnp.stack([jnp.where(core == 0, mine, other), jnp.where(core == 0, other, mine)])
        picked = jnp.stack([pick(blocks, index[i], 2) for i in range(3 * rounds)])
        picked = picked.reshape(3 * GROUP_HEADS, HD, width)
        return jnp.pad(picked, ((0, 0), (0, LANES - HD), (0, 0))).reshape(3 * GROUP_LANES, width)

    def body(index_ref, mine_ref, other_ref, out_ref):
        for head in range(3 * GROUP_HEADS):
            out_ref[head * LANES + HD : (head + 1) * LANES, :] = jnp.zeros((LANES - HD, width), LOW)

        def fill(first, second):
            for unit in range(3 * rounds):
                slot = index_ref[unit]
                for part in range(2 * copies):
                    row = (2 * copies * unit + part) * rows
                    start = row // HD * LANES + row % HD
                    source = second if part // copies else first
                    out_ref[start : start + rows, :] = source[part % copies, slot]

        own = index_ref[3 * rounds]

        @pl.when(own == 0)
        def _():
            fill(mine_ref, other_ref)

        @pl.when(own == 1)
        def _():
            fill(other_ref, mine_ref)

    spec = pl.BlockSpec((3 * GROUP_LANES, width), lambda *_: (0, 0))
    return call(
        body,
        (1,),
        (jnp.concatenate([index, core.reshape(1)]),),
        [(mine, whole_block(mine)), (other, whole_block(other))],
        [(like(3 * GROUP_LANES, width), spec)],
        cost=(0, 0, 0),
    )[0]


def assemble_blocks(sources, targets, rows, width):
    each = len(targets) // len(sources)

    def body(start_ref, *refs):
        for number in range(len(targets)):
            place = number % each
            refs[-1][start_ref[number]] = refs[number // each][place * rows : (place + 1) * rows, :]

    shape = jax.ShapeDtypeStruct((len(targets), rows, width), LOW)
    return call(
        body,
        (1,),
        (jnp.stack(targets).astype(jnp.int32),),
        [(array, whole_block(array)) for array in sources],
        [(shape, whole_block(shape))],
        cost=(0, 0, 0),
    )[0]


def assemble(sources, targets, rows, shape, after=()):
    places = [(part, i) for part, source in enumerate(sources) for i in range(source.shape[0] // rows)]
    if rows % 16:
        out = jnp.zeros(shape, LOW)
        for (part, i), target in zip(places, targets, strict=True):
            out = lax.dynamic_update_slice(out, sources[part][i * rows : (i + 1) * rows], (target * rows, 0))
        return out

    def body(start_ref, *refs):
        for number, (part, i) in enumerate(places):
            start = pl.multiple_of(start_ref[number] * rows, 16)
            refs[-1][pl.ds(start, rows), :] = refs[part][i * rows : (i + 1) * rows, :]

    return call(
        body,
        (1,),
        (jnp.stack(targets).astype(jnp.int32),),
        [(array, whole_block(array)) for array in sources],
        [(like(*shape), pl.BlockSpec(shape, lambda *_: (0, 0)))],
        cost=(0, 0, 0),
        after=after,
    )[0]


def on_device(
    hidden_states,
    clip_lengths,
    norm_gains,
    norm_shifts,
    proj_biases,
    up_bias,
    in_proj,
    out_proj,
    up_proj,
    down_proj,
    cotangent,
):
    tokens_here, width = hidden_states.shape
    fsdp_count = lax.axis_size("fsdp")
    dp_count = lax.axis_size("dp")
    fsdp_index = lax.axis_index("fsdp")
    dp_index = lax.axis_index("dp")
    core = dp_index % 2
    copies = dp_count // 2
    copy_index = dp_index // 2
    region = (dp_index * fsdp_count + fsdp_index) // CLIP_DEV
    place = fsdp_index % CLIP_DEV
    length = lax.dynamic_index_in_dim(clip_lengths, region, keepdims=False)
    span = tokens_here * CLIP_DEV
    hidden_units = up_bias.shape[0]
    positions = jnp.arange(tokens_here, dtype=jnp.int32)
    row_valid = (place * tokens_here + positions < length).astype(jnp.float32)
    copy_levels = copies.bit_length() - 1
    fsdp_levels = fsdp_count.bit_length() - 1
    far_count = fsdp_count // 2
    half = width // 2

    core_bit = ("dp", 1, core)
    copy_bits = [("dp", 2 << level, copy_index >> level & 1) for level in reversed(range(copy_levels))]
    fsdp_bits = [("fsdp", 1 << level, fsdp_index >> level & 1) for level in reversed(range(fsdp_levels))]
    far_bits, near_bit = fsdp_bits[:-1], fsdp_bits[-1]
    lap_bits = fsdp_bits[:-2]
    orders = [[near_bit] + copy_bits, copy_bits + [near_bit]]
    stages = len(orders[0])
    token = jnp.zeros((8, LANES), jnp.float32)

    def by_core(first, second):
        return jnp.where(core == 0, first, second)

    def swap_stage(value, number):
        return swap_by_core(value, orders[0][number][:2], orders[1][number][:2])

    def own_bit(number):
        return by_core(orders[0][number][2], orders[1][number][2])

    def block_index(bits):
        indices = []
        for order in orders:
            near, copy = 0, 0
            for (axis, mask, _), bit in zip(order, bits, strict=True):
                near, copy = (bit, copy) if axis == "fsdp" else (near, copy + bit * (mask // 2))
            indices.append(near * copies + copy)
        return by_core(*indices)

    def all_bits(count):
        return [[number >> (count - 1 - i) & 1 for i in range(count)] for number in range(1 << count)]

    def gathered_targets(other_core):
        targets = []
        for differs in all_bits(len(far_bits) + stages):
            differs = differs[::-1]
            upper = 0
            for (_, mask, mine), bit in zip(far_bits, differs, strict=False):
                upper += (mine ^ bit) * (mask // 2)
            indices = []
            for order in orders:
                near, copy = 0, 0
                for (axis, mask, mine), bit in zip(order, differs[len(far_bits) :], strict=True):
                    near, copy = (mine ^ bit, copy) if axis == "fsdp" else (near, copy + (mine ^ bit) * (mask // 2))
                indices.append((2 * upper + near) * copies + copy)
            targets.append(by_core(*(indices[::-1] if other_core else indices)))
        return targets

    def stage_swap(value, number):
        if number < len(far_bits):
            return swap(value, *far_bits[number][:2])
        return swap_stage(value, number - len(far_bits))

    def first_blocks(grad):
        rest = all_bits(stages - 1)
        sent = [pick(grad, block_index([1 - own_bit(0)] + bits), 1) for bits in rest]
        kept = [pick(grad, block_index([own_bit(0)] + bits), 1) for bits in rest]
        return jnp.stack(sent, axis=1), kept

    def add_low(kept, came):
        return (kept.astype(jnp.float32) + came.astype(jnp.float32)).astype(LOW)

    def first_sum(kept, came):
        came = came if isinstance(came, list) else [came[:, i] for i in range(len(kept))]
        return jnp.stack([add_low(block, other) for block, other in zip(kept, came, strict=True)], axis=1)

    def next_start(held, number):
        pair = held.reshape(held.shape[:1] + (2, held.shape[1] // 2) + held.shape[2:])
        return pick(pair, own_bit(number), 1), swap_stage(pick(pair, 1 - own_bit(number), 1), number)

    def next_end(kept, came):
        held = add_low(kept, came)
        for number in range(2, stages):
            held = add_low(*next_start(held, number))
        return held.reshape(held.shape[:1] + held.shape[2:])

    out_rows = out_proj.shape[0] // dp_count
    shard_units = up_proj.shape[0]
    half_units = shard_units // 2
    up_rows = half_units // copies
    down_rows = down_proj.shape[0] // copies
    out_piece = pick(pick(out_proj.reshape(copies, 2, out_rows, width), copy_index), core)
    up_piece = pick(pick(up_proj.reshape(2, copies, up_rows, width), core), copy_index)
    up_held = jnp.concatenate([up_piece, out_piece])
    down_piece = pick(down_proj.reshape(copies, down_rows, hidden_units), copy_index)
    down_held = split_columns(down_piece, core, fsdp_count)
    far_stages = len(far_bits)

    def gather_stages(held, came, first, last):
        for number in range(first + 1, last + 1):
            held = jnp.concatenate([held, came])
            came = stage_swap(held, number)
        return held, came

    rounds = fsdp_count // CLIP_DEV
    unit_rows = in_proj.shape[0] // 3
    half_rows = unit_rows // 2
    piece_rows = unit_rows // dp_count
    pair_pairs, single_pairs, single_first = [], [], []
    slot_table = [[0] * (3 * rounds) for _ in range(CLIP_DEV)]
    pair_laps, single_laps = [0] * CLIP_DEV, [0] * CLIP_DEV
    for source in range(fsdp_count):
        keys = [divmod(3 * source + slot, fsdp_count) for slot in range(3)]
        owners = [spot // rounds for _, spot in keys]
        single = 0 if owners[0] != owners[1] else 2
        single_first.append(single == 0)
        twins = [1, 2] if single == 0 else [0, 1]
        place_of = owners[twins[0]]
        pair_pairs.append((source, pair_laps[place_of] * CLIP_DEV + place_of))
        for number, slot in enumerate(twins):
            kind, spot = keys[slot]
            slot_table[place_of][kind * rounds + spot % rounds] = pair_laps[place_of] * 3 + number
        pair_laps[place_of] += 1
        place_of = owners[single]
        single_pairs.append((source, single_laps[place_of] * CLIP_DEV + place_of))
        kind, spot = keys[single]
        slot_table[place_of][kind * rounds + spot % rounds] = single_laps[place_of] * 3 + 2
        single_laps[place_of] += 1
    single_leads = pick(jnp.array(single_first, jnp.int32), fsdp_index)
    slot_row = pick(jnp.array(slot_table, jnp.int32), place)
    key_table = [[row.index(slot) for slot in range(3 * rounds)] for row in slot_table]
    key_row = pick(jnp.array(key_table, jnp.int32), place)

    with jax.named_scope("gather_in_proj"):
        units = pick(pick(in_proj.reshape(3, 2, copies, piece_rows, width), core, 1), copy_index, 1)
        twins = lax.ppermute(lax.dynamic_slice_in_dim(units, single_leads, 2, 0), "fsdp", pair_pairs)
        single = lax.ppermute(lax.dynamic_slice_in_dim(units, 2 - 2 * single_leads, 1, 0), "fsdp", single_pairs)
    token, twins, single, own_x, own_grad = fence(token, [], twins, single, hidden_states, cotangent)

    with jax.named_scope("gather_tokens"):
        near = swap(own_x, "fsdp", 1)
        far = swap(own_x, "fsdp", 2)
    with jax.named_scope("gather_in_proj"):
        units = jnp.concatenate([twins, single])
        units = widen_bits(units.reshape((1,) * len(lap_bits) + units.shape), lap_bits, 0)
        units = units.reshape((1,) * copy_levels + (3 * rounds, piece_rows, width))
        units = widen_bits(units, copy_bits, 0).reshape(copies, 3 * rounds, piece_rows, width)
    token, units, near, far, own_grad, up_held, down_held = fence(
        token, [], units, near, far, own_grad, up_held, down_held
    )

    with jax.named_scope("gather_in_proj"):
        core_came = swap(units, *core_bit[:2])
    with jax.named_scope("gather_tokens"):
        both = swap(far, "fsdp", 1)
    with jax.named_scope("gather_up_and_out_proj"):
        up_came = stage_swap(up_held, 0)
    with jax.named_scope("gather_in_proj"):
        weight_in = spread_heads(units, core_came, core, slot_row, rounds)
    clip_blocks = [hidden_states, near, far, None]

    padded_width = 3 * GROUP_LANES
    zeros = jnp.zeros((width,), jnp.float32)
    group_bias = jnp.stack([proj_biases[0] * SCORE_SCALE, zeros, proj_biases[1]])
    group_bias = pick(group_bias.reshape(3, CLIP_DEV, GROUP_HEADS, HD), place, 1)
    group_bias = jnp.pad(group_bias, ((0, 0), (0, 0), (0, LANES - HD)))
    lane = jnp.arange(LANES)
    spare = jnp.stack(
        [
            lane == HD,
            (lane > HD) & (lane <= HD + 3),
            (lane >= HD) & (lane < HD + 3),
        ]
    ).astype(jnp.float32)
    columns = (group_bias + spare[:, None]).reshape(1, padded_width)

    def project_block(number, held, after):
        limit = (length - (place ^ number) * tokens_here).reshape(1)
        return project(
            number, clip_blocks[number], weight_in, norm_gains[0:1], norm_shifts[0:1], columns, limit, held, after
        )

    held = project_block(0, None, [token])
    held = project_block(1, held, [token])
    token, up_came, own_grad, down_held = fence(token, [held[0]], up_came, own_grad, down_held)
    with jax.named_scope("gather_down_proj"):
        down_came = stage_swap(down_held, 0)
    with jax.named_scope("gather_up_and_out_proj"):
        up_held, up_came = gather_stages(up_held, up_came, 0, far_stages - 1)
    with jax.named_scope("gather_tokens"):
        grad_other = swap(own_grad, "dp", 1)
    held = project_block(2, held, [token])
    token, both, grad_other = fence(token, [held[0]], both, grad_other)
    clip_blocks[3] = both
    queries, pair, normed_one = project_block(3, held, [token])
    token, pair, up_came = fence(token, [], pair, up_came)
    with jax.named_scope("gather_up_and_out_proj"):
        up_held, up_came = gather_stages(up_held, up_came, far_stages - 1, far_stages)
    contexts, ready = [None] * CLIP_DEV, [None] * CLIP_DEV
    contexts[1], ready[1] = attend(1, queries, pair, [token])
    token, contexts[1], down_came = fence(token, [], contexts[1], down_came)
    with jax.named_scope("context_back"):
        sent_one = swap(contexts[1], "fsdp", 1)
    with jax.named_scope("gather_down_proj"):
        down_held, down_came = gather_stages(down_held, down_came, 0, far_stages - 1)
    contexts[3], ready[3] = attend(3, queries, pair, [token])
    token, contexts[3], sent_one, up_came = fence(token, [], contexts[3], sent_one, up_came)
    with jax.named_scope("context_back"):
        sent_three = swap(contexts[3], "fsdp", 3)
    with jax.named_scope("gather_out_proj"):
        up_held, up_came = gather_stages(up_held, up_came, far_stages, far_stages + stages - 2)
        blocks = jnp.concatenate([up_held, up_came]).reshape(-1, up_rows + out_rows, width)
        up_held = blocks[:, :up_rows].reshape(-1, width)
        out_held = blocks[:, up_rows:].reshape(-1, width)
        out_came = stage_swap(out_held, far_stages + stages - 1)
    contexts[2], ready[2] = attend(2, queries, pair, [token])
    token, contexts[2], sent_three, out_came, up_held, down_came = fence(
        token, [], contexts[2], sent_three, out_came, up_held, down_came
    )
    with jax.named_scope("context_back"):
        sent_two = swap(contexts[2], "fsdp", 2)
    with jax.named_scope("gather_up_proj"):
        rows = up_held.shape[0] // 2
        up_came = [stage_swap(up_held[i * rows : (i + 1) * rows], far_stages + stages - 1) for i in range(2)]
    with jax.named_scope("gather_out_proj"):
        out_blocks = jnp.concatenate([out_held, out_came])
        out_other = swap(out_blocks, *core_bit[:2])
    contexts[0], ready[0] = attend(0, queries, pair, [token])
    token, sent_two, out_other, down_came, up_came[0] = fence(
        token, [contexts[0]], sent_two, out_other, down_came, up_came[0]
    )
    with jax.named_scope("gather_out_proj"):
        targets, others = gathered_targets(False), gathered_targets(True)
        homes = [2 * t + core for t in targets] + [2 * t + 1 - core for t in others]
        out_full = assemble_blocks([out_blocks, out_other], homes, out_rows, width).reshape(width, width)
    with jax.named_scope("context_back"):
        parts = jnp.stack([contexts[0], sent_one, sent_two, sent_three])
        context_low = jnp.concatenate([pick(parts, place ^ group) for group in range(CLIP_DEV)], axis=1)
    context_heads = jnp.concatenate(contexts)
    queries_ready = jnp.concatenate(ready)
    with jax.named_scope("gather_down_proj"):
        down_held, down_came = gather_stages(down_held, down_came, far_stages - 1, far_stages)
    with jax.named_scope("gather_up_proj"):
        up_half = assemble([up_held, *up_came], targets, up_rows, (hidden_units // 2, width))

    inputs = hidden_states.astype(jnp.float32)
    grad_pair = jnp.concatenate([cotangent, grad_other])
    attention = dot_nt(context_low, out_full) + proj_biases[2]
    middle = inputs + attention
    unit_two, scale_two = normalise(middle)
    normed_two = (unit_two * norm_gains[1] + norm_shifts[1]).astype(LOW)
    normed_other = swap(normed_two, "dp", 1)
    half_bias = pick(up_bias.reshape(fsdp_count, 2, half_units), core, 1).reshape(hidden_units // 2)
    token, normed_two, down_came = fence(token, [], normed_two, down_came)
    held = list(widen(0, normed_two, up_half, half_bias, None, [token]))
    with jax.named_scope("gather_down_proj"):
        down_held, down_came = gather_stages(down_held, down_came, far_stages, far_stages + stages - 1)
    activated, slope = widen(1, normed_other, up_half, half_bias, held)
    normed_pair = jnp.concatenate([normed_two, normed_other])
    grad_down = dot_tn(grad_pair, activated).astype(LOW)
    with jax.named_scope("reduce_down_proj"):
        grad = grad_down.reshape(far_count, 2 * copies, down_rows, hidden_units // 2)
        sent, down_kept = first_blocks(grad)
        sent = [sent[:, i] for i in range(len(down_kept))]
    token, slope, down_came, *sent = fence(token, [], slope, down_came, *sent)

    with jax.named_scope("reduce_down_proj"):
        down_first = [swap_stage(block, 0) for block in sent]
    with jax.named_scope("gather_down_proj"):
        down_half = assemble([down_held, down_came], targets, down_rows, (width, hidden_units // 2), [token])
    grad_activated = dot_nn(grad_pair, down_half)
    grad_widened = (grad_activated * slope.astype(jnp.float32)).astype(LOW)
    token, grad_widened, down_first[0] = fence(token, [], grad_widened, down_first[0])

    def over_cores(rows, product):
        sent = product(rows[tokens_here:]).astype(LOW)
        return product(rows[:tokens_here]) + swap(sent, "dp", 1).astype(jnp.float32)

    grad_normed_two = over_cores(grad_widened, lambda rows: dot_nn(rows, up_half))
    grad_out = cotangent.astype(jnp.float32)
    grad_middle = grad_out + norm_back(grad_normed_two, norm_gains[1], unit_two, scale_two)
    grad_attention = grad_middle.astype(LOW)
    grad_context = dot_nn(grad_attention, out_full).astype(LOW)
    token, grad_context, grad_widened, *down_first = fence(token, [], grad_context, grad_widened, *down_first)

    with jax.named_scope("grad_context_to_heads"):
        groups = [grad_context[:, i * GROUP_WIDTH : (i + 1) * GROUP_WIDTH] for i in range(CLIP_DEV)]
        groups = jnp.stack(groups)
        sends = [pick(groups, place ^ j) for j in range(CLIP_DEV)]
        grad_came = [swap(sends[j], "fsdp", j) for j in range(1, CLIP_DEV)]
    grad_up = dot_tn(grad_widened, normed_pair).astype(LOW)
    grad_exit = dot_tn(grad_attention, context_low).astype(LOW)
    feedforward = over_cores(activated, lambda rows: dot_nt(rows, down_half)) + proj_biases[3]
    outputs = (middle + feedforward).astype(LOW)
    stat_terms = jnp.stack(
        [
            jnp.sum(row_valid * jnp.sum(middle * middle, axis=1)),
            jnp.sum(row_valid * jnp.sum(attention * attention, axis=1)),
            jnp.sum(row_valid * jnp.sum(feedforward * feedforward, axis=1)),
        ]
    )
    with jax.named_scope("small_sums"):
        half_up = jnp.sum(grad_widened.astype(jnp.float32), axis=0).reshape(fsdp_count, half_units)
        up_terms = jnp.zeros((fsdp_count, 2, half_units), jnp.float32)
        up_terms = lax.dynamic_update_index_in_dim(up_terms, half_up, core, 1).reshape(hidden_units // width, width)
        early = jnp.concatenate(
            [
                jnp.stack(
                    [
                        jnp.sum(grad_normed_two * unit_two, axis=0),
                        jnp.sum(grad_normed_two, axis=0),
                        jnp.sum(grad_attention.astype(jnp.float32), axis=0),
                        jnp.sum(grad_out, axis=0),
                        jnp.pad(stat_terms, (0, width - 3)),
                    ]
                ),
                up_terms,
            ]
        )
    token, *grad_came, grad_up, grad_exit, down_first[0] = fence(
        token, [], *grad_came, grad_up, grad_exit, down_first[0]
    )

    grad_heads = jnp.concatenate([sends[0], *grad_came])
    far_split = (2,) * len(far_bits)
    with jax.named_scope("reduce_up_proj"):
        exit_grad = grad_exit.reshape(far_count * 2 * copies, 2, out_rows, width)
        exit_came = give(exit_grad, 1, core_bit)
        sent, up_kept = first_blocks(grad_up.reshape(far_count, 2 * copies, up_rows, width))
        up_first = swap_stage(sent, 0)
    with jax.named_scope("reduce_down_proj"):
        down_kept, down_came = next_start(first_sum(down_kept, down_first), 1)
    held = attend_back(0, queries_ready, pair, context_heads, grad_heads, None, [token])
    token, exit_came = fence(token, [held[0]], exit_came)

    with jax.named_scope("reduce_up_proj"):
        exit_grad = keep(exit_grad, exit_came, 1, core_bit).reshape(far_count, 2 * copies, out_rows, width)
        sent, exit_kept = first_blocks(exit_grad)
        exit_first = swap_stage(sent, 0)
    held = attend_back(1, queries_ready, pair, context_heads, grad_heads, held, [token])
    token, down_came = fence(token, [held[0]], down_came)

    with jax.named_scope("reduce_down_proj"):
        down_sum = next_end(down_kept, down_came)
        down_sum = down_sum.reshape(far_split + down_sum.shape[1:])
        down_came = give(down_sum, far_stages - 1, far_bits[-1])
    held = attend_back(2, queries_ready, pair, context_heads, grad_heads, held, [token])
    token, up_first, exit_first, down_came = fence(token, [held[0]], up_first, exit_first, down_came)

    with jax.named_scope("reduce_up_proj"):
        up_second = jnp.concatenate([first_sum(up_kept, up_first), first_sum(exit_kept, exit_first)], axis=2)
        up_kept, up_came = next_start(up_second, 1)
    with jax.named_scope("reduce_down_proj"):
        down_sum = keep(down_sum, down_came, far_stages - 1, far_bits[-1])
        if far_stages > 2:
            down_sum = reduce_last(down_sum, far_bits[1:-1])
        down_came = give(down_sum, 0, far_bits[0])
    kinds = attend_back(3, queries_ready, pair, context_heads, grad_heads, held, [token])
    token, *kinds, up_came, down_came = fence(token, [], *kinds, up_came, down_came)

    grad_query, grad_key, grad_value = kinds
    with jax.named_scope("reduce_up_proj"):
        up_second = next_end(up_kept, up_came)
        up_second = up_second.reshape(far_split + up_second.shape[1:])
        up_came = give(up_second, far_stages - 1, far_bits[-1])
    with jax.named_scope("reduce_in_proj"):
        entry = jnp.stack([dot_tn(grad, normed_one).astype(LOW) for grad in kinds])
        entry = entry.reshape(3, GROUP_HEADS, LANES, width)[:, :, :HD]
        entry = entry.reshape((3 * rounds, 2) + (2,) * copy_levels + (piece_rows, width))
    with jax.named_scope("reduce_down_proj"):
        down_sum = keep(down_sum, down_came, 0, far_bits[0])
        down_sum = down_sum.reshape((1,) * copy_levels + down_sum.shape)
        down_came = swap(down_sum, *copy_bits[0][:2])
    token, entry, down_came = fence(token, [], entry, down_came)
    with jax.named_scope("reduce_in_proj"):
        entry_came = give(entry, 1, core_bit)
    with jax.named_scope("reduce_down_proj"):
        down_sum = join_bit(down_sum, down_came, 0, copy_bits[0][2])
        down_sum = widen_bits(down_sum, copy_bits[1:], 1).reshape(down_rows * copies, hidden_units // 2)
        down_other = swap(down_sum, *core_bit[:2])
    partial, sums = [None] * CLIP_DEV, [None] * CLIP_DEV
    partial[3], sums[3] = entry_back(3, clip_blocks[3], kinds, weight_in, [token])
    token, partial[3], entry_came = fence(token, [], partial[3], entry_came)
    with jax.named_scope("reduce_tokens"):
        both_came = swap(partial[3], "fsdp", 1)
    with jax.named_scope("reduce_in_proj"):
        entry = keep(entry, entry_came, 1, core_bit).reshape(3 * rounds, half_rows, width)
        entry = gather_blocks(entry, key_row)
        entry = entry.reshape((2,) * len(lap_bits) + (3, half_rows, width))
        if len(lap_bits) > 1:
            entry = reduce_last(entry, lap_bits[1:])
        entry_came = give(entry, 0, lap_bits[0])
    partial[1], sums[1] = entry_back(1, clip_blocks[1], kinds, weight_in, [token])
    token, partial[1], up_came = fence(token, [], partial[1], up_came)
    with jax.named_scope("reduce_tokens"):
        near_came = swap(partial[1], "fsdp", 1)
    partial[2], sums[2] = entry_back(2, clip_blocks[2], kinds, weight_in, [token])
    partial[0], sums[0] = entry_back(0, clip_blocks[0], kinds, weight_in, [token])
    token, partial[2], partial[0], sums[0], entry_came, down_other, both_came, up_came = fence(
        token, [], partial[2], partial[0], sums[0], entry_came, down_other, both_came, up_came
    )
    with jax.named_scope("reduce_tokens"):
        far_came = swap(add_low(partial[2], both_came), "fsdp", 2)
    with jax.named_scope("reduce_in_proj"):
        entry = keep(entry, entry_came, 0, lap_bits[0])
        entry = entry.reshape((3,) + (2,) * copy_levels + (piece_rows, width))
        entry_came = give(entry, 1, copy_bits[0])
    with jax.named_scope("reduce_up_proj"):
        sums_up = keep(up_second, up_came, far_stages - 1, far_bits[-1])
        if far_stages > 2:
            sums_up = reduce_last(sums_up, far_bits[1:-1])
        up_came = give(sums_up, 0, far_bits[0])
    down_out = merge_columns(down_sum, down_other, core, fsdp_count)
    token, entry_came = fence(token, [], entry_came)
    with jax.named_scope("reduce_in_proj"):
        entry = keep(entry, entry_came, 1, copy_bits[0])
        entry = reduce_bits(entry, copy_bits[1:], 1)
        twins = lax.ppermute(entry[:2], "fsdp", [(target, source) for source, target in pair_pairs])
        single = lax.ppermute(entry[2:], "fsdp", [(target, source) for source, target in single_pairs])
    def place_heads(grads):
        columns = jnp.sum(grads.astype(jnp.float32), axis=0).reshape(GROUP_HEADS, LANES)[:, :HD]
        rows = jnp.zeros((CLIP_DEV, GROUP_WIDTH), jnp.float32)
        return lax.dynamic_update_index_in_dim(rows, columns.reshape(GROUP_WIDTH), place, 0).reshape(width)

    with jax.named_scope("small_sums"):
        late = jnp.concatenate(
            [
                sums[0] + sums[1] + sums[2] + sums[3],
                jnp.stack([place_heads(grad_query), place_heads(grad_value)]),
                early,
            ]
        )
        for level in range(dp_count.bit_length() - 1):
            late = late + swap(late, "dp", 1 << level)
        late = late + swap(late, "fsdp", 1)
    token, twins, single, near_came, far_came, late, up_came = fence(
        token, [], twins, single, near_came, far_came, late, up_came
    )
    with jax.named_scope("reduce_up_proj"):
        sums_up = keep(sums_up, up_came, 0, far_bits[0])
        ends = widen_bits(sums_up.reshape((1,) * copy_levels + sums_up.shape), copy_bits, 0)
        ends = widen_bits(ends[None], [core_bit], 0).reshape(2, copies, -1, width)
        up_sum = ends[:, :, :up_rows].reshape(up_proj.shape).astype(jnp.float32)
        exit_sum = jnp.moveaxis(ends[:, :, up_rows : up_rows + out_rows], 0, 1)
        exit_sum = exit_sum.reshape(out_proj.shape).astype(jnp.float32)
    with jax.named_scope("reduce_in_proj"):
        entry = jnp.where(
            single_leads == 1, jnp.concatenate([single, twins]), jnp.concatenate([twins, single])
        ).reshape(3 * piece_rows, width)
        entry = widen_bits(entry.reshape((1,) * (1 + copy_levels) + entry.shape), copy_bits, 1)
        entry = widen_bits(entry, [core_bit], 0).reshape(dp_count, 3, piece_rows, width)
        entry_sum = jnp.moveaxis(entry, 1, 0).reshape(in_proj.shape).astype(jnp.float32)

    with jax.named_scope("small_sums"):
        for level in range(1, fsdp_levels):
            late = late + swap(late, "fsdp", 1 << level)
    grad_normed_one = partial[0].astype(jnp.float32) + near_came.astype(jnp.float32) + far_came.astype(jnp.float32)
    unit_one, scale_one = normalise(inputs)
    grad_hidden = grad_middle + norm_back(grad_normed_one, norm_gains[0], unit_one, scale_one)
    valid_count = jnp.sum(clip_lengths).astype(jnp.float32) * width
    root_means = jnp.sqrt(late[14, :3] / valid_count)
    return (
        outputs,
        grad_hidden.astype(LOW),
        entry_sum,
        exit_sum,
        up_sum,
        down_out,
        jnp.stack([late[0], late[10]]),
        jnp.stack([late[1], late[11]]),
        jnp.stack([late[8], late[9], late[12], late[13]]),
        late[15 : 15 + hidden_units // width].reshape(hidden_units),
        root_means,
    )


def solution(mesh):
    in_specs = (
        P(("dp", "fsdp"), None),
        P(),
        P(),
        P(),
        P(),
        P(),
        P("fsdp", None),
        P("fsdp", None),
        P("fsdp", None),
        P("fsdp", None),
        P(("dp", "fsdp"), None),
    )
    out_specs = (
        P(("dp", "fsdp"), None),
        P(("dp", "fsdp"), None),
        P("fsdp", None),
        P("fsdp", None),
        P("fsdp", None),
        P("fsdp", None),
        P(),
        P(),
        P(),
        P(),
        P(),
    )
    return jax.shard_map(
        on_device, mesh=mesh, in_specs=in_specs, out_specs=out_specs, check_vma=False
    )
```
